512 devices in a mesh: resp: 128 (over z, y, core), section: 4 (over x).
Axes of the slice: x: 4, y: 8, z: 8, core: 2. Of those that a mesh axis runs over, the one named last changes fastest.
Arguments:
- queries: bfloat16 [4, 16384, 4096], P('section', 'resp'), may hold values from -6 to 6
- out_grad: bfloat16 [4, 16384, 4096], P('section', 'resp'), may hold values from -18 to 18
- resp_kv: bfloat16 [4, 16384, 1024], P('section', 'resp'), may hold values from -6 to 6
- prompt_kv: bfloat16 [4, 512, 128, 1024], P('section', 'resp'), may hold values from -6 to 6
- prompt_hidden: bfloat16 [4, 4096, 4096], P('section', 'resp'), may hold values from -6 to 6
- norm_gain: bfloat16 [4, 4096], P('section'), may hold values from 0.25 to 1.75
- kv_weight: bfloat16 [4, 4096, 1024], P('section', 'resp'), may hold values from -0.09375 to 0.09375
- upper_grad: bfloat16 [4096, 4096], P('resp'), may hold values from -3 to 3
- group_list: int32 [512], replicated, may hold values from 0 to 31, as said below
- lengths: int32 [512], P('resp'), may hold values from 1 to 32
- owner_map: int32 [32, 128], replicated, may hold values from 0 to 127, each once within a row
Outputs:
- query_grad: bfloat16 [4, 16384, 4096], P('section', 'resp')
- resp_kv_grad: bfloat16 [4, 16384, 1024], P('section', 'resp')
- prompt_grad: bfloat16 [4, 4096, 4096], P('section', 'resp')
The draws below stay inside these ranges and needn't reach their ends.
Inputs may be any that keep to these rules, and one draw needn't show every extreme that they name: `group_list`: each of the 32 prompts is named by exactly 16 responses. `owner_map`: each row names every index of resp once.
All inputs are finite; a program needn't handle non-finite values.
Results may differ from the reference program's by a relative error of at most 0.025.
Values may be sent and summed in bfloat16 or wider, within the bound.
No kernel may reach another device: no remote copies, remote signals or barrier semaphores. Data moves between devices by JAX's collectives and lax.ppermute only.
A program may use at most 64 MiB of HBM per device.

```python
import jax
import jax.numpy as jnp
from jax import lax

D = 4096
QH = 32
KVH = 4
HD = 128
GROUP = 16
PLEN = 128
RLEN = 32
RESP_DEV = 4
RESPONSES = 512
NPROMPT = 32
PAGE_ROWS = 1
PROWS = 4096
N_RESP = 128
N_SECTION = 4


def shared_signs(key):
    sign_key = jax.random.fold_in(key, 97)
    flips = jax.random.bernoulli(sign_key, 0.5, (N_SECTION, RESPONSES, KVH, HD))
    return jnp.where(flips, 1.0, -1.0).astype(jnp.float32)


def draw_queries(key, part):
    signs = shared_signs(key)
    key = jax.random.fold_in(key, 5)
    base_key, row_key, power_key = jax.random.split(key, 3)
    per_group = QH // KVH
    shape = (N_SECTION, RESPONSES, RLEN, KVH, per_group, HD)
    base = jnp.clip(jax.random.normal(base_key, shape, jnp.float32), -6.0, 6.0)
    picks = jax.random.randint(row_key, (N_SECTION, RESPONSES, 3, 1), 0, RLEN, dtype=jnp.int32)
    row_ids = jnp.arange(RLEN, dtype=jnp.int32)
    chosen = jnp.any(picks == row_ids, axis=2) | (row_ids == 0)
    levels = jax.random.randint(power_key, (N_SECTION, RESPONSES, RLEN, KVH, per_group, 1), 3, 7, dtype=jnp.int32)
    aligned = levels.astype(jnp.float32) * signs[:, :, None, :, None, :]
    drawn = jnp.where(chosen[:, :, :, None, None, None], aligned, base)
    return drawn.reshape(N_SECTION, RESPONSES * RLEN, QH * HD).astype(jnp.bfloat16)


def draw_prompt_kv(key, part):
    signs = shared_signs(key)
    key = jax.random.fold_in(key, 7)
    base_key, place_key, gap_key = jax.random.split(key, 3)
    shape = (N_SECTION, RESPONSES, PLEN, 2, KVH, HD)
    base = jnp.clip(jax.random.normal(base_key, shape, jnp.float32), -6.0, 6.0)
    first = jax.random.randint(place_key, (N_SECTION, RESPONSES, 1, KVH), 0, PLEN, dtype=jnp.int32)
    second = (first + jax.random.randint(gap_key, (N_SECTION, RESPONSES, 1, KVH), 1, PLEN, dtype=jnp.int32)) % PLEN
    positions = jnp.arange(PLEN, dtype=jnp.int32)[None, None, :, None]
    lowered = jnp.where(jnp.arange(HD, dtype=jnp.int32) < HD // 12, 5.5, 6.0).astype(jnp.float32)
    top_key = 6.0 * signs[:, :, None]
    near_key = lowered * signs[:, :, None]
    keys_part = jnp.where((positions == second)[..., None], near_key, base[:, :, :, 0])
    keys_part = jnp.where((positions == first)[..., None], top_key, keys_part)
    drawn = jnp.stack([keys_part, base[:, :, :, 1]], axis=3)
    return drawn.reshape(N_SECTION, RESPONSES, PLEN, 2 * KVH * HD).astype(jnp.bfloat16)


def draw_group_list(key, part):
    first_key = jax.random.fold_in(key, 11)
    shuffled = jax.random.permutation(first_key, RESPONSES)
    return (shuffled // GROUP).astype(jnp.int32)


def draw_lengths(key, part):
    base_key = jax.random.fold_in(key, 23)
    first_key, second_key, third_key = jax.random.split(base_key, 3)
    drawn_lengths = jax.random.randint(first_key, (RESPONSES,), 1, RLEN + 1, dtype=jnp.int32)
    longest = jax.random.randint(second_key, (), 0, RESPONSES, dtype=jnp.int32)
    offset = jax.random.randint(third_key, (), 1, RESPONSES, dtype=jnp.int32)
    shortest = (longest + offset) % RESPONSES
    drawn_lengths = drawn_lengths.at[longest].set(RLEN)
    return drawn_lengths.at[shortest].set(1)


def steps_of(own_key, dims, cuts, low, largest):
    def one(axis_at, parts):
        steps = jax.random.uniform(jax.random.fold_in(jax.random.fold_in(own_key, 6), axis_at), (parts,), jnp.float32, low / len(cuts), largest / len(cuts))
        return jnp.repeat(jnp.exp(steps), dims[axis_at] // parts).reshape((-1,) + (1,) * (len(dims) - axis_at - 1))

    factor_of = one(*cuts[0])
    for cut in cuts[1:]:
        factor_of = factor_of * one(*cut)
    return factor_of


def normal_values(rng, extent, width, limit, shards=(), held_as=jnp.bfloat16):
    level = steps_of(rng, extent, shards, -0.22, 0.18) if shards else 1.0
    entries = jax.random.normal(rng, extent, jnp.float32) * width * level
    return jnp.minimum(jnp.maximum(entries, -limit), limit).astype(held_as)


def setup_inputs(seed: int = 0) -> dict:
    key_list = jax.random.split(jax.random.key(seed), 12)
    queries = draw_queries(jax.random.fold_in(key_list[11], 71), 0)
    out_grad = normal_values(key_list[1], (N_SECTION, RESPONSES * RLEN, QH * HD), 3.0, 18.0, ((0, 4), (1, 128)))
    resp_kv = normal_values(key_list[2], (N_SECTION, RESPONSES * RLEN, 2 * KVH * HD), 1.0, 6.0, ((0, 4), (1, 128)))
    prompt_kv = draw_prompt_kv(jax.random.fold_in(key_list[11], 71), 0)
    prompt_hidden = normal_values(key_list[4], (N_SECTION, PROWS, D), 1.0, 6.0, ((0, 4), (1, 128)))
    norm_gain = jnp.clip(1.0 + 0.15 * jax.random.normal(key_list[5], (N_SECTION, D), jnp.float32), 0.25, 1.75).astype(jnp.bfloat16)
    kv_weight = normal_values(key_list[6], (N_SECTION, D, 2 * KVH * HD), D ** -0.5, 0.09375, ((0, 4), (1, 128)))
    upper_grad = normal_values(key_list[7], (PROWS, D), 0.5, 3.0, ((0, 128),))
    group_list = draw_group_list(jax.random.fold_in(key_list[11], 71), 0)
    lengths = draw_lengths(jax.random.fold_in(key_list[11], 71), 0)
    owner_map = jax.vmap(lambda own: jax.random.permutation(own, N_RESP))(jax.random.split(key_list[10], NPROMPT)).reshape((NPROMPT, N_RESP)).astype(jnp.int32)
    return {"queries": queries, "out_grad": out_grad, "resp_kv": resp_kv, "prompt_kv": prompt_kv, "prompt_hidden": prompt_hidden, "norm_gain": norm_gain, "kv_weight": kv_weight, "upper_grad": upper_grad, "group_list": group_list, "lengths": lengths, "owner_map": owner_map}


def product(pattern, first_op, second_op):
    return jnp.einsum(pattern, first_op.astype(jnp.float32), second_op.astype(jnp.float32))

def response_backward(resp_queries, resp_out_grad, own_kv, cached_kv, resp_lengths):
    batch_size = resp_queries.shape[0]
    resp_rows = resp_queries.shape[1]
    prompt_len = cached_kv.shape[1]
    per_group = QH // KVH
    kv_width = KVH * HD
    scaling = HD ** (-0.5)
    shaped = resp_queries.reshape(batch_size, resp_rows, KVH, per_group, HD)
    all_keys = jnp.concatenate([cached_kv[:, :, :kv_width], own_kv[:, :, :kv_width]], axis=1)
    all_keys = all_keys.reshape(batch_size, prompt_len + resp_rows, KVH, HD)
    all_values = jnp.concatenate([cached_kv[:, :, kv_width:], own_kv[:, :, kv_width:]], axis=1)
    all_values = all_values.reshape(batch_size, prompt_len + resp_rows, KVH, HD)
    scores = product('bqkgd,bckd->bkgqc', shaped, all_keys) * scaling
    query_pos = jnp.arange(resp_rows, dtype=jnp.int32)[:, None]
    key_pos = jnp.arange(prompt_len + resp_rows, dtype=jnp.int32)[None, :] - prompt_len
    allowed = (key_pos < 0)[None] | (key_pos <= query_pos)[None] & (key_pos[None] < resp_lengths[:, None, None])
    scores = jnp.where(allowed[:, None, None], scores, -1e+30)
    highest = lax.optimization_barrier(jnp.max(scores, axis=-1, keepdims=True))
    expo_terms = jnp.exp(scores - highest)
    softmax = expo_terms / lax.optimization_barrier(jnp.sum(expo_terms, axis=-1, keepdims=True))
    live_rows = (jnp.arange(resp_rows, dtype=jnp.int32)[None, :] < resp_lengths[:, None]).astype(resp_out_grad.dtype)
    masked = resp_out_grad.reshape(batch_size, resp_rows, KVH, per_group, HD) * live_rows[:, :, None, None, None]
    rounded = softmax.astype(jnp.bfloat16)
    attn_out = product('bkgqc,bckd->bqkgd', rounded, all_values)
    delta = jnp.einsum('bqkgd,bqkgd->bkgq', masked.astype(jnp.float32), attn_out)
    prob_grad = product('bqkgd,bckd->bkgqc', masked, all_values)
    score_grad = (scaling * softmax * (prob_grad - delta[..., None])).astype(jnp.bfloat16)
    query_part = product('bkgqc,bckd->bqkgd', score_grad, all_keys).reshape(batch_size, resp_rows, QH * HD)
    key_grad = product('bkgqc,bqkgd->bckd', score_grad, shaped).reshape(batch_size, prompt_len + resp_rows, kv_width)
    value_grad = product('bkgqc,bqkgd->bckd', rounded, masked).reshape(batch_size, prompt_len + resp_rows, kv_width)
    both_grads = jnp.concatenate([key_grad, value_grad], axis=-1)
    return (query_part, both_grads[:, prompt_len:], both_grads[:, :prompt_len])

def reference(queries, out_grad, resp_kv, prompt_kv, prompt_hidden, norm_gain, kv_weight, upper_grad, group_list, lengths, owner_map):
    full_width = 2 * KVH * HD
    prompt_ids = jnp.arange(NPROMPT, dtype=jnp.int32)
    query_outs = []
    own_outs = []
    terms = []
    for section_index in range(N_SECTION):
        items = (queries[section_index].reshape(N_RESP, RESP_DEV, RLEN, QH * HD), out_grad[section_index].reshape(N_RESP, RESP_DEV, RLEN, QH * HD), resp_kv[section_index].reshape(N_RESP, RESP_DEV, RLEN, full_width), prompt_kv[section_index].reshape(N_RESP, RESP_DEV, PLEN, full_width), group_list.reshape(N_RESP, RESP_DEV), lengths.reshape(N_RESP, RESP_DEV))

        def one_block(totals, block_items):
            block_q, block_out, block_kv, block_prompt, block_groups, block_lengths = block_items
            query_part, own_part, prompt_part = response_backward(block_q, block_out, block_kv, block_prompt, block_lengths)
            low_part = lax.optimization_barrier(prompt_part.astype(jnp.bfloat16))
            select = (block_groups[:, None] == prompt_ids[None, :]).astype(jnp.float32)
            totals = totals + jnp.einsum('jn,jpx->npx', select, low_part.astype(jnp.float32), precision=lax.Precision.HIGHEST)
            return (totals, (query_part.astype(jnp.bfloat16), own_part.astype(jnp.bfloat16)))
        start_totals = jnp.zeros((NPROMPT, PLEN, full_width), jnp.float32)
        totals, (query_part, own_part) = lax.scan(one_block, start_totals, items)
        query_outs.append(query_part.reshape(RESPONSES * RLEN, QH * HD))
        own_outs.append(own_part.reshape(RESPONSES * RLEN, full_width))
        page_total = totals.astype(jnp.bfloat16).reshape(NPROMPT, N_RESP, PAGE_ROWS, full_width)
        stored = jnp.zeros((N_RESP, NPROMPT, PAGE_ROWS, full_width), jnp.bfloat16)
        stored = stored.at[owner_map, prompt_ids[:, None]].set(page_total).reshape(PROWS, full_width)
        normed_grad = jnp.dot(stored, kv_weight[section_index].T, preferred_element_type=jnp.float32)
        hidden = prompt_hidden[section_index].astype(jnp.float32)
        gain = norm_gain[section_index].astype(jnp.float32)
        inverse = lax.rsqrt(lax.optimization_barrier(jnp.mean(hidden * hidden, axis=-1, keepdims=True)) + 1e-06)
        scaled = gain[None, :] * normed_grad
        term = inverse * scaled - hidden * inverse ** 3 * lax.optimization_barrier(jnp.mean(hidden * scaled, axis=-1, keepdims=True))
        terms.append(term)
    running = upper_grad.astype(jnp.float32)
    prompt_outs = [None] * N_SECTION
    for section_index in reversed(range(N_SECTION)):
        running = running + terms[section_index]
        prompt_outs[section_index] = running.astype(jnp.bfloat16)
    return (jnp.stack(query_outs), jnp.stack(own_outs), jnp.stack(prompt_outs))
```

```python
import functools

import jax
import jax.numpy as jnp
from jax import lax
from jax.experimental import pallas as pl
from jax.experimental.pallas import tpu as pltpu
from jax.sharding import PartitionSpec as P

QH = 32
KVH = 4
HD = 128
PER = QH // KVH
RESP_DEV = 4
WIDE = 2 * KVH * HD
LOG2E = 1.4426950408889634
SMALL = pltpu.CompilerParams(vmem_limit_bytes=16 * 1024 * 1024)
F32 = jnp.float32
BF16 = jnp.bfloat16


def dot(a, b, dims):
    return lax.dot_general(a, b, (dims, ((), ())), preferred_element_type=F32)


RESP_AXES = ("z", "y", "core")
LANES = 128


def resp_index():
    index = 0
    for axis in RESP_AXES:
        index = index * lax.axis_size(axis) + lax.axis_index(axis)
    return index


def attention_kernel(groups, lengths, q_ref, do_ref, own_ref, cache_ref, owner_ref, dq_ref, down_ref, send_ref, mixed_ref):
    b = pl.program_id(0)
    count = RESP_DEV
    length = lengths[b]
    rows = q_ref.shape[0]
    plen = cache_ref.shape[0]
    scaling = HD ** (-0.5)
    lanes = PER * rows
    key_pos = lax.broadcasted_iota(jnp.int32, (rows, lanes), 0)
    query_pos = lax.broadcasted_iota(jnp.int32, (rows, lanes), 1) % rows
    allowed = (key_pos <= query_pos) & (key_pos < length)
    live = (lax.broadcasted_iota(jnp.int32, (rows, HD), 0) < length).astype(BF16)
    group = groups[resp_index() * count + b]
    owners = owner_ref[pl.ds(group, 1), :]
    devices = owner_ref.shape[1]
    place = (lax.broadcasted_iota(jnp.int32, (devices, devices), 0) == owners).astype(BF16)
    own_kv = own_ref[...]
    cached = cache_ref[...]
    heads = [slice(h * HD, (h + 1) * HD) for h in range(QH)]
    key_cols = heads[:KVH]
    value_cols = heads[KVH : 2 * KVH]
    each = range(KVH)
    q = [jnp.concatenate([q_ref[:, h] for h in heads[k * PER : (k + 1) * PER]], axis=0) for k in each]
    keys = [jnp.concatenate([cached[:, at], own_kv[:, at]], axis=0) for at in key_cols]
    scores = [dot(keys[k], q[k], ((1,), (1,))) for k in each]
    do = [jnp.concatenate([do_ref[:, h] * live for h in heads[k * PER : (k + 1) * PER]], axis=0) for k in each]
    values = [jnp.concatenate([cached[:, at], own_kv[:, at]], axis=0) for at in value_cols]
    prob_grad = [dot(values[k], do[k], ((1,), (1,))) for k in each]
    low, score_grad = [], []
    for k in each:
        masked = jnp.concatenate([scores[k][:plen], jnp.where(allowed, scores[k][plen:], -1e30)], axis=0)
        expo = jnp.exp2((masked - jnp.max(masked, axis=0, keepdims=True)) * (scaling * LOG2E))
        probs = expo * (1.0 / jnp.sum(expo, axis=0, keepdims=True))
        low.append(probs.astype(BF16))
        delta = jnp.sum(probs * prob_grad[k], axis=0, keepdims=True)
        score_grad.append((probs * ((prob_grad[k] - delta) * scaling)).astype(BF16))
    grads = []
    for k in each:
        grads.append((k, 1, value_cols[k], dot(low[k], do[k], ((1,), (0,)))))
        grads.append((k, 0, key_cols[k], dot(score_grad[k], q[k], ((1,), (0,)))))
    for k in each:
        dq = dot(score_grad[k], keys[k], ((0,), (0,)))
        for g, h in enumerate(heads[k * PER : (k + 1) * PER]):
            dq_ref[:, h] = dq[g * rows : (g + 1) * rows].astype(BF16)
    for k, half, at, grad in grads:
        down_ref[:, at] = grad[plen:].astype(BF16)
        part = dot(place, grad[:plen].astype(BF16), ((1,), (0,)))
        mixed_ref[k, pl.ds(2 * b + half, devices, stride=2 * count), :] = part

    @pl.when(b == count - 1)
    def _():
        for k in range(KVH):
            send_ref[:, k * HD : (k + 1) * HD] = mixed_ref[k].astype(BF16)


def attention(queries, out_grad, resp_kv, prompt_kv, group_list, lengths, owner_map):
    count, plen, _ = prompt_kv.shape
    total = queries.shape[0]
    rows = total // count
    width = queries.shape[1]
    by_resp = lambda w: pl.BlockSpec((rows, w), lambda b, *_: (b, 0))
    return pl.pallas_call(
        attention_kernel,
        grid_spec=pltpu.PrefetchScalarGridSpec(
            num_scalar_prefetch=2,
            grid=(count,),
            in_specs=[
                by_resp(width),
                by_resp(width),
                by_resp(WIDE),
                pl.BlockSpec((None, plen, WIDE), lambda b, *_: (b, 0, 0)),
                pl.BlockSpec(owner_map.shape, lambda b, *_: (0, 0)),
            ],
            out_specs=[
                by_resp(width),
                by_resp(WIDE),
                pl.BlockSpec((2 * count * plen, WIDE // 2), lambda b, *_: (0, 0)),
            ],
            scratch_shapes=[pltpu.VMEM((KVH, 2 * count * plen, HD), F32)],
        ),
        out_shape=[
            jax.ShapeDtypeStruct((total, width), BF16),
            jax.ShapeDtypeStruct((total, WIDE), BF16),
            jax.ShapeDtypeStruct((2 * count * plen, WIDE // 2), BF16),
        ],
        cost_estimate=pl.CostEstimate(flops=10**9, bytes_accessed=6 * 10**6, transcendentals=700000),
        name="attention_backward",
    )(group_list, lengths, queries, out_grad, resp_kv, prompt_kv, owner_map)


def page_kernel(groups_ref, arrived_ref, page_ref):
    copies, prompts, _ = page_ref.shape
    rows, half = arrived_ref.shape
    ids = lax.broadcasted_iota(jnp.int32, (2 * prompts, rows), 0)
    odd = lax.broadcasted_iota(jnp.int32, (2 * prompts, rows), 1) % 2
    select = (ids == groups_ref[...] + prompts * odd).astype(BF16)
    page = dot(select, arrived_ref[...], ((1,), (0,))).astype(BF16)
    for copy in range(copies):
        page_ref[copy, :, :half] = page[:prompts]
        page_ref[copy, :, half:] = page[prompts:]


def natural_order(transposed):
    span = 2 * LANES
    held = lax.broadcasted_iota(jnp.int32, (span, span), 1 if transposed else 0)
    model = lax.broadcasted_iota(jnp.int32, (span, span), 0 if transposed else 1)
    rows = 32
    core, rest = held // LANES, held % LANES
    return (model == rest // rows * (2 * rows) + core * rows + rest % rows).astype(BF16)


def collect_kernel(*refs):
    out_ref, pieces = refs[-1], refs[:-1]
    rows = len(pieces)
    for k, ref in enumerate(pieces):
        out_ref[lax.rem(lax.axis_index("y") + rows - k, rows)] = ref[...]


def project_kernel(pages_ref, own_ref, other_ref, gain_ref, out_ref, gain_rows):
    gain_rows[...] = dot(gain_ref[...], natural_order(True), ((1,), (0,)))
    pairs = out_ref.shape[1] // (2 * LANES)
    gain = [gain_rows[pl.ds(lax.axis_index("z") * pairs + pair, 1), :] for pair in range(pairs)]
    first = lax.axis_index("core") == 0
    own = dot(pages_ref[...], own_ref[...], ((1,), (1,)))
    other = dot(pages_ref[...], other_ref[...], ((1,), (1,)))
    for core in range(2):
        normed = jnp.where(first, own, other) if core == 0 else jnp.where(first, other, own)
        for pair in range(pairs):
            at = slice(pair * LANES, (pair + 1) * LANES)
            start = (core * pairs + pair) * LANES
            scale = gain[pair][:, core * LANES : (core + 1) * LANES]
            out_ref[:, start : start + LANES] = (normed[:, at] * scale).astype(BF16)


def term_kernel(scaled_ref, hidden_ref, *refs):
    got, (out_ref, term_ref, layers_ref) = refs[:-3], refs[-3:]
    blocks, rows, cols = scaled_ref.shape
    sections, step, width = layers_ref.shape
    here = lax.axis_index("section")
    layers_ref[here] = hidden_ref[here].astype(F32)
    for k, ref in enumerate(got, 1):
        layers_ref[lax.rem(here + sections - k, sections)] = ref[...].astype(F32)
    span = 2 * LANES
    pairs = cols // span
    mixed = []
    for block in range(blocks):
        for pair in range(pairs):
            low, high = pair * LANES, (pairs + pair) * LANES
            mixed.append(
                jnp.concatenate([scaled_ref[block, :, low : low + LANES], scaled_ref[block, :, high : high + LANES]], axis=1)
            )
    scaled = dot(jnp.concatenate(mixed, axis=0), natural_order(False), ((1,), (0,)))
    squares = jnp.zeros((rows, span), F32)
    cross = jnp.zeros((rows, span), F32)
    for n in range(len(mixed)):
        at = slice(n * span, (n + 1) * span)
        part = scaled[n * rows : (n + 1) * rows]
        term_ref[:, at] = part
        hidden = layers_ref[:, :, at].reshape(rows, span)
        squares += hidden * hidden
        cross += hidden * part
    inverse = lax.rsqrt(jnp.sum(squares, axis=-1, keepdims=True) / width + 1e-06)
    back = inverse**3 * (jnp.sum(cross, axis=-1, keepdims=True) / width)
    chunk = 4 * LANES
    for start in range(0, width, chunk):
        at = slice(start, start + chunk)
        term = inverse * term_ref[:, at] - layers_ref[:, :, at].reshape(rows, chunk) * back
        sums = [term[(sections - 1) * step :]]
        for s in reversed(range(sections - 1)):
            sums.insert(0, sums[0] + term[s * step : (s + 1) * step])
        out_ref[:, at] = jnp.concatenate(sums, axis=0).astype(BF16)


def finish(pages, weights, hidden, norm_gain, upper_grad):
    prompt_count, width = upper_grad.shape
    sections, quarter, _ = hidden[0].shape
    members = pages.shape[0]
    pages = lax.all_to_all(pages, "z", split_axis=0, concat_axis=0, tiled=True)
    scaled = pl.pallas_call(
        project_kernel,
        out_shape=jax.ShapeDtypeStruct((members * prompt_count, width // members), BF16),
        scratch_shapes=[pltpu.VMEM((width // (2 * LANES), 2 * LANES), F32)],
        compiler_params=SMALL,
        cost_estimate=pl.CostEstimate(flops=3 * 10**8, bytes_accessed=2 * 10**6, transcendentals=0),
        name="projection",
    )(pages.reshape(-1, WIDE), *weights, norm_gain.reshape(-1, 2 * LANES))
    scaled = scaled.reshape(members * sections, quarter, -1)
    scaled = lax.all_to_all(scaled, ("z", "section"), split_axis=0, concat_axis=0, tiled=True)
    sums = pl.pallas_call(
        term_kernel,
        out_shape=jax.ShapeDtypeStruct((prompt_count, width), BF16),
        scratch_shapes=[pltpu.VMEM((prompt_count, width), F32), pltpu.VMEM((sections, quarter, width), F32)],
        compiler_params=SMALL,
        cost_estimate=pl.CostEstimate(flops=10**8, bytes_accessed=10**6, transcendentals=0),
        name="norm_terms",
    )(scaled.reshape(members, prompt_count, -1), *hidden)
    sums = lax.all_to_all(sums.reshape(sections, quarter, width), "section", split_axis=0, concat_axis=0, tiled=True)
    return (upper_grad.astype(F32) + sums.reshape(prompt_count, width).astype(F32)).astype(BF16)


def turn(piece, axis, k):
    size = lax.axis_size(axis)
    return lax.ppermute(piece, axis, [(i, (i + k) % size) for i in range(size)])


def shift(rows, axis):
    size, here = rows.shape[0], lax.axis_index(axis)
    return [turn(lax.dynamic_index_in_dim(rows, lax.rem(here + k, size), keepdims=False), axis, k) for k in range(1, size)]


def body(queries, out_grad, resp_kv, prompt_kv, prompt_hidden, norm_gain, kv_weight, upper_grad, group_list, lengths, owner_map):
    prompt_count, devices = owner_map.shape
    sections = lax.axis_size("section")
    width = prompt_hidden.shape[-1]
    query_out, own_out, outgoing = attention(
        queries[0], out_grad[0], resp_kv[0], prompt_kv[0], group_list, lengths, owner_map
    )
    outgoing, weight = lax.optimization_barrier((outgoing, kv_weight[0]))
    outgoing = outgoing.reshape(devices, -1, WIDE // 2)
    incoming = lax.all_to_all(outgoing, RESP_AXES, split_axis=0, concat_axis=0, tiled=True)
    weights = [weight] + [turn(weight, "y", k) for k in range(1, lax.axis_size("y"))]
    weights = pl.pallas_call(
        collect_kernel,
        out_shape=jax.ShapeDtypeStruct((len(weights),) + weight.shape, BF16),
        compiler_params=SMALL,
        cost_estimate=pl.CostEstimate(flops=0, bytes_accessed=10**6, transcendentals=0),
        name="weight_rows",
    )(*weights)
    hidden = prompt_hidden[0].reshape(sections, prompt_count // sections, width)
    incoming, hidden, weights = lax.optimization_barrier((incoming, hidden, weights))
    pages = pl.pallas_call(
        page_kernel,
        out_shape=jax.ShapeDtypeStruct((lax.axis_size("z"), prompt_count, WIDE), BF16),
        compiler_params=SMALL,
        cost_estimate=pl.CostEstimate(flops=10**8, bytes_accessed=10**6, transcendentals=0),
        name="page_sum",
    )(jnp.repeat(group_list, 2)[None, :], incoming.reshape(-1, WIDE // 2))
    weights = weights.reshape(-1, WIDE)
    weights = [weights, lax.ppermute(weights, "core", [(0, 1), (1, 0)])]
    hidden = [hidden] + shift(hidden, "section")
    prompt_out = finish(pages, weights, hidden, norm_gain, upper_grad)
    return (query_out[None], own_out[None], prompt_out[None])


def solution(mesh):
    wide = jax.sharding.Mesh(mesh.devices.reshape(8, 8, 2, mesh.shape["section"]), RESP_AXES + ("section",))
    in_specs = (
        P("section", RESP_AXES, None),
        P("section", RESP_AXES, None),
        P("section", RESP_AXES, None),
        P("section", RESP_AXES, None, None),
        P("section", RESP_AXES, None),
        P("section", None),
        P("section", RESP_AXES, None),
        P(RESP_AXES, None),
        P(),
        P(RESP_AXES),
        P(),
    )
    out_specs = (P("section", RESP_AXES, None),) * 3
    return jax.shard_map(body, mesh=wide, in_specs=in_specs, out_specs=out_specs, check_vma=False)
```

```python
import functools

import jax
import jax.numpy as jnp
from jax import lax
from jax.experimental import pallas as pl
from jax.experimental.pallas import tpu as pltpu
from jax.sharding import PartitionSpec as P

QH = 32
KVH = 4
HD = 128
PER = QH // KVH
RESP_DEV = 4
WIDE = 2 * KVH * HD
LOG2E = 1.4426950408889634
SMALL = pltpu.CompilerParams(vmem_limit_bytes=16 * 1024 * 1024)
F32 = jnp.float32
BF16 = jnp.bfloat16


def dot(a, b, dims):
    return lax.dot_general(a, b, (dims, ((), ())), preferred_element_type=F32)


RESP_AXES = ("z", "y", "core")
LANES = 128


def resp_index():
    index = 0
    for axis in RESP_AXES:
        index = index * lax.axis_size(axis) + lax.axis_index(axis)
    return index


def attention_kernel(groups, lengths, q_ref, do_ref, own_ref, cache_ref, owner_ref, dq_ref, down_ref, send_ref, mixed_ref):
    b = pl.program_id(0)
    count = RESP_DEV
    length = lengths[b]
    rows = q_ref.shape[0]
    plen = cache_ref.shape[0]
    scaling = HD ** (-0.5)
    lanes = PER * rows
    key_pos = lax.broadcasted_iota(jnp.int32, (rows, lanes), 0)
    query_pos = lax.broadcasted_iota(jnp.int32, (rows, lanes), 1) % rows
    allowed = (key_pos <= query_pos) & (key_pos < length)
    live = (lax.broadcasted_iota(jnp.int32, (rows, HD), 0) < length).astype(BF16)
    group = groups[resp_index() * count + b]
    owners = owner_ref[pl.ds(group, 1), :]
    devices = owner_ref.shape[1]
    place = (lax.broadcasted_iota(jnp.int32, (devices, devices), 0) == owners).astype(BF16)
    own_kv = own_ref[...]
    cached = cache_ref[...]
    heads = [slice(h * HD, (h + 1) * HD) for h in range(QH)]
    key_cols = heads[:KVH]
    value_cols = heads[KVH : 2 * KVH]
    each = range(KVH)
    q = [jnp.concatenate([q_ref[:, h] for h in heads[k * PER : (k + 1) * PER]], axis=0) for k in each]
    keys = [jnp.concatenate([cached[:, at], own_kv[:, at]], axis=0) for at in key_cols]
    scores = [dot(keys[k], q[k], ((1,), (1,))) for k in each]
    do = [jnp.concatenate([do_ref[:, h] * live for h in heads[k * PER : (k + 1) * PER]], axis=0) for k in each]
    values = [jnp.concatenate([cached[:, at], own_kv[:, at]], axis=0) for at in value_cols]
    prob_grad = [dot(values[k], do[k], ((1,), (1,))) for k in each]
    low, score_grad = [], []
    for k in each:
        masked = jnp.concatenate([scores[k][:plen], jnp.where(allowed, scores[k][plen:], -1e30)], axis=0)
        expo = jnp.exp2((masked - jnp.max(masked, axis=0, keepdims=True)) * (scaling * LOG2E))
        probs = expo * (1.0 / jnp.sum(expo, axis=0, keepdims=True))
        low.append(probs.astype(BF16))
        delta = jnp.sum(low[k].astype(F32) * prob_grad[k], axis=0, keepdims=True)
        score_grad.append((probs * ((prob_grad[k] - delta) * scaling)).astype(BF16))
    grads = []
    for k in each:
        grads.append((k, 1, value_cols[k], dot(low[k], do[k], ((1,), (0,)))))
        grads.append((k, 0, key_cols[k], dot(score_grad[k], q[k], ((1,), (0,)))))
    for k in each:
        dq = dot(score_grad[k], keys[k], ((0,), (0,)))
        for g, h in enumerate(heads[k * PER : (k + 1) * PER]):
            dq_ref[:, h] = dq[g * rows : (g + 1) * rows].astype(BF16)
    for k, half, at, grad in grads:
        down_ref[:, at] = grad[plen:].astype(BF16)
        part = dot(place, grad[:plen].astype(BF16), ((1,), (0,)))
        mixed_ref[k, pl.ds(2 * b + half, devices, stride=2 * count), :] = part

    @pl.when(b == count - 1)
    def _():
        for k in range(KVH):
            send_ref[:, k * HD : (k + 1) * HD] = mixed_ref[k].astype(BF16)


def attention(queries, out_grad, resp_kv, prompt_kv, group_list, lengths, owner_map):
    count, plen, _ = prompt_kv.shape
    total = queries.shape[0]
    rows = total // count
    width = queries.shape[1]
    by_resp = lambda w: pl.BlockSpec((rows, w), lambda b, *_: (b, 0))
    return pl.pallas_call(
        attention_kernel,
        grid_spec=pltpu.PrefetchScalarGridSpec(
            num_scalar_prefetch=2,
            grid=(count,),
            in_specs=[
                by_resp(width),
                by_resp(width),
                by_resp(WIDE),
                pl.BlockSpec((None, plen, WIDE), lambda b, *_: (b, 0, 0)),
                pl.BlockSpec(owner_map.shape, lambda b, *_: (0, 0)),
            ],
            out_specs=[
                by_resp(width),
                by_resp(WIDE),
                pl.BlockSpec((2 * count * plen, WIDE // 2), lambda b, *_: (0, 0)),
            ],
            scratch_shapes=[pltpu.VMEM((KVH, 2 * count * plen, HD), F32)],
        ),
        out_shape=[
            jax.ShapeDtypeStruct((total, width), BF16),
            jax.ShapeDtypeStruct((total, WIDE), BF16),
            jax.ShapeDtypeStruct((2 * count * plen, WIDE // 2), BF16),
        ],
        cost_estimate=pl.CostEstimate(flops=10**9, bytes_accessed=6 * 10**6, transcendentals=700000),
        name="attention_backward",
    )(group_list, lengths, queries, out_grad, resp_kv, prompt_kv, owner_map)


def page_kernel(groups_ref, arrived_ref, page_ref):
    copies, prompts, _ = page_ref.shape
    rows, half = arrived_ref.shape
    ids = lax.broadcasted_iota(jnp.int32, (2 * prompts, rows), 0)
    odd = lax.broadcasted_iota(jnp.int32, (2 * prompts, rows), 1) % 2
    select = (ids == groups_ref[...] + prompts * odd).astype(BF16)
    page = dot(select, arrived_ref[...], ((1,), (0,))).astype(BF16)
    for copy in range(copies):
        page_ref[copy, :, :half] = page[:prompts]
        page_ref[copy, :, half:] = page[prompts:]


def natural_order(transposed):
    span = 2 * LANES
    held = lax.broadcasted_iota(jnp.int32, (span, span), 1 if transposed else 0)
    model = lax.broadcasted_iota(jnp.int32, (span, span), 0 if transposed else 1)
    rows = 32
    core, rest = held // LANES, held % LANES
    return (model == rest // rows * (2 * rows) + core * rows + rest % rows).astype(BF16)


def collect_kernel(*refs):
    out_ref, pieces = refs[-1], refs[:-1]
    block, at = out_ref.shape[1], 0
    for ref in pieces:
        for start in range(0, ref.shape[0], block):
            out_ref[at] = ref[start : start + block]
            at += 1


def project_kernel(pages_ref, own_ref, sibling_ref, near_ref, far_ref, gain_ref, out_ref, gain_rows, weight_ref):
    span = 2 * LANES
    gain = gain_ref[...].astype(F32)
    gain = jnp.concatenate([gain[:, start : start + span] for start in range(0, gain.shape[1], span)], axis=0)
    gain_rows[...] = dot(gain.astype(BF16), natural_order(True), ((1,), (0,)))
    cores, rows, block, _ = weight_ref.shape
    core, row = lax.axis_index("core"), lax.axis_index("y")
    other = 1 - core
    weight_ref[core, row] = own_ref[...]
    weight_ref[other, row] = sibling_ref[...]
    for j in range(1, rows // 2):
        below = lax.rem(row + rows - j, rows)
        above = lax.rem(row + j, rows)
        near = jnp.where(core == 0, below, above)
        far = jnp.where(core == 0, above, below)
        weight_ref[core, near] = near_ref[2 * j - 2]
        weight_ref[other, near] = near_ref[2 * j - 1]
        weight_ref[other, far] = far_ref[2 * j - 2]
        weight_ref[core, far] = far_ref[2 * j - 1]
    middle = lax.rem(row + rows // 2, rows)
    weight_ref[core, middle] = near_ref[rows - 2]
    weight_ref[other, middle] = far_ref[rows - 2]
    cols = rows * block
    pairs = cols // LANES
    scales = [gain_rows[pl.ds(lax.axis_index("z") * pairs + pair, 1), :] for pair in range(pairs)]
    for c in range(cores):
        normed = dot(pages_ref[...], weight_ref[c].reshape(cols, WIDE), ((1,), (1,)))
        for pair in range(pairs):
            at = slice(pair * LANES, (pair + 1) * LANES)
            start = c * cols + pair * LANES
            out_ref[:, start : start + LANES] = (normed[:, at] * scales[pair][:, c * LANES : (c + 1) * LANES]).astype(BF16)


def term_kernel(scaled_ref, hidden_ref, *refs):
    got, (out_ref, term_ref, layers_ref) = refs[:-3], refs[-3:]
    blocks, rows, cols = scaled_ref.shape
    sections, step, width = layers_ref.shape
    here = lax.axis_index("section")
    layers_ref[here] = hidden_ref[here].astype(F32)
    for k, ref in enumerate(got, 1):
        layers_ref[lax.rem(here + sections - k, sections)] = ref[...].astype(F32)
    span = 2 * LANES
    pairs = cols // span
    mixed = []
    for block in range(blocks):
        for pair in range(pairs):
            low, high = pair * LANES, (pairs + pair) * LANES
            mixed.append(
                jnp.concatenate([scaled_ref[block, :, low : low + LANES], scaled_ref[block, :, high : high + LANES]], axis=1)
            )
    scaled = dot(jnp.concatenate(mixed, axis=0), natural_order(False), ((1,), (0,)))
    squares = jnp.zeros((rows, span), F32)
    cross = jnp.zeros((rows, span), F32)
    for n in range(len(mixed)):
        at = slice(n * span, (n + 1) * span)
        part = scaled[n * rows : (n + 1) * rows]
        term_ref[:, at] = part
        hidden = layers_ref[:, :, at].reshape(rows, span)
        squares += hidden * hidden
        cross += hidden * part
    inverse = lax.rsqrt(jnp.sum(squares, axis=-1, keepdims=True) / width + 1e-06)
    back = inverse**3 * (jnp.sum(cross, axis=-1, keepdims=True) / width)
    chunk = 4 * LANES
    for start in range(0, width, chunk):
        at = slice(start, start + chunk)
        term = inverse * term_ref[:, at] - layers_ref[:, :, at].reshape(rows, chunk) * back
        sums = [term[(sections - 1) * step :]]
        for s in reversed(range(sections - 1)):
            sums.insert(0, sums[0] + term[s * step : (s + 1) * step])
        out_ref[:, at] = jnp.concatenate(sums, axis=0).astype(BF16)


def finish(pages, weights, hidden, norm_gain, upper_grad):
    prompt_count, width = upper_grad.shape
    sections, quarter, _ = hidden[0].shape
    members = pages.shape[0]
    scaled = pl.pallas_call(
        project_kernel,
        out_shape=jax.ShapeDtypeStruct((members * prompt_count, width // members), BF16),
        scratch_shapes=[
            pltpu.VMEM((width // (2 * LANES), 2 * LANES), F32),
            pltpu.VMEM((2, lax.axis_size("y")) + weights[0].shape, BF16),
        ],
        compiler_params=SMALL,
        cost_estimate=pl.CostEstimate(flops=3 * 10**8, bytes_accessed=2 * 10**6, transcendentals=0),
        name="projection",
    )(pages.reshape(-1, WIDE), *weights, norm_gain)
    scaled = scaled.reshape(members * sections, quarter, -1)
    scaled = lax.all_to_all(scaled, ("z", "section"), split_axis=0, concat_axis=0, tiled=True)
    sums = pl.pallas_call(
        term_kernel,
        out_shape=jax.ShapeDtypeStruct((prompt_count, width), BF16),
        scratch_shapes=[pltpu.VMEM((prompt_count, width), F32), pltpu.VMEM((sections, quarter, width), F32)],
        compiler_params=SMALL,
        cost_estimate=pl.CostEstimate(flops=10**8, bytes_accessed=10**6, transcendentals=0),
        name="norm_terms",
    )(scaled.reshape(members, prompt_count, -1), *hidden)
    sums = lax.all_to_all(sums.reshape(sections, quarter, width), "section", split_axis=0, concat_axis=0, tiled=True)
    return (upper_grad.astype(F32) + sums.reshape(prompt_count, width).astype(F32)).astype(BF16)


def swap(piece):
    return lax.ppermute(piece, "core", [(0, 1), (1, 0)])


def turn(piece, axis, k):
    size = lax.axis_size(axis)
    return lax.ppermute(piece, axis, [(i, (i + k) % size) for i in range(size)])


def part_ways(piece, j):
    rows = lax.axis_size("y")
    pairs = [(2 * y + c, (y + (j if c == 0 else rows - j)) % rows * 2 + c) for y in range(rows) for c in range(2)]
    return lax.ppermute(piece, ("y", "core"), pairs)


def hand_over(hidden, k):
    size, here = hidden.shape[0], lax.axis_index("section")
    return turn(lax.dynamic_index_in_dim(hidden, lax.rem(here + k, size), keepdims=False), "section", k)


def gather_rows(weight, sibling):
    rows = lax.axis_size("y")
    both = jnp.concatenate([weight, sibling], axis=0)
    pieces = [part_ways(both, j) for j in range(1, rows // 2)] + [turn(weight, "y", rows // 2)]
    return pl.pallas_call(
        collect_kernel,
        out_shape=jax.ShapeDtypeStruct((rows - 1,) + weight.shape, BF16),
        compiler_params=SMALL,
        cost_estimate=pl.CostEstimate(flops=0, bytes_accessed=10**6, transcendentals=0),
        name="weight_rows",
    )(*pieces)


def body(queries, out_grad, resp_kv, prompt_kv, prompt_hidden, norm_gain, kv_weight, upper_grad, group_list, lengths, owner_map):
    prompt_count, devices = owner_map.shape
    sections = lax.axis_size("section")
    width = prompt_hidden.shape[-1]
    weight = kv_weight[0]
    sibling = swap(weight)
    hidden = prompt_hidden[0].reshape(sections, prompt_count // sections, width)
    query_out, own_out, outgoing = attention(
        queries[0], out_grad[0], resp_kv[0], prompt_kv[0], group_list, lengths, owner_map
    )
    outgoing, weight, sibling, hidden = lax.optimization_barrier((outgoing, weight, sibling, hidden))
    outgoing = outgoing.reshape(devices, -1, WIDE // 2)
    incoming = lax.all_to_all(outgoing, RESP_AXES, split_axis=0, concat_axis=0, tiled=True)
    near = gather_rows(weight, sibling)
    layers = [hidden, hand_over(hidden, 1)]
    incoming, near, layers = lax.optimization_barrier((incoming, near, layers))
    pages = pl.pallas_call(
        page_kernel,
        out_shape=jax.ShapeDtypeStruct((lax.axis_size("z"), prompt_count, WIDE), BF16),
        compiler_params=SMALL,
        cost_estimate=pl.CostEstimate(flops=10**8, bytes_accessed=10**6, transcendentals=0),
        name="page_sum",
    )(jnp.repeat(group_list, 2)[None, :], incoming.reshape(-1, WIDE // 2))
    pages = lax.all_to_all(pages, "z", split_axis=0, concat_axis=0, tiled=True)
    far = swap(near)
    layers += [hand_over(layers[0], k) for k in range(2, sections)]
    pages, far, layers = lax.optimization_barrier((pages, far, layers))
    prompt_out = finish(pages, [weight, sibling, near, far], layers, norm_gain, upper_grad)
    return (query_out[None], own_out[None], prompt_out[None])


def solution(mesh):
    wide = jax.sharding.Mesh(mesh.devices.reshape(8, 8, 2, mesh.shape["section"]), RESP_AXES + ("section",))
    in_specs = (
        P("section", RESP_AXES, None),
        P("section", RESP_AXES, None),
        P("section", RESP_AXES, None),
        P("section", RESP_AXES, None, None),
        P("section", RESP_AXES, None),
        P("section", None),
        P("section", RESP_AXES, None),
        P(RESP_AXES, None),
        P(),
        P(RESP_AXES),
        P(),
    )
    out_specs = (P("section", RESP_AXES, None),) * 3
    return jax.shard_map(body, mesh=wide, in_specs=in_specs, out_specs=out_specs, check_vma=False)
```

```python
import functools

import jax
import jax.numpy as jnp
from jax import lax
from jax.experimental import pallas as pl
from jax.experimental.pallas import tpu as pltpu
from jax.sharding import PartitionSpec as P

QH = 32
KVH = 4
HD = 128
PER = QH // KVH
RESP_DEV = 4
WIDE = 2 * KVH * HD
LOG2E = 1.4426950408889634
SMALL = pltpu.CompilerParams(vmem_limit_bytes=16 * 1024 * 1024)
F32 = jnp.float32
BF16 = jnp.bfloat16


def dot(a, b, dims):
    return lax.dot_general(a, b, (dims, ((), ())), preferred_element_type=F32)


RESP_AXES = ("z", "y", "core")
LANES = 128


def resp_index():
    index = 0
    for axis in RESP_AXES:
        index = index * lax.axis_size(axis) + lax.axis_index(axis)
    return index


def attention_kernel(groups, lengths, q_ref, do_ref, own_ref, cache_ref, owner_ref, dq_ref, down_ref, send_ref, mixed_ref):
    b = pl.program_id(0)
    count = RESP_DEV
    length = lengths[b]
    rows = q_ref.shape[0]
    plen = cache_ref.shape[0]
    scaling = HD ** (-0.5)
    lanes = PER * rows
    key_pos = lax.broadcasted_iota(jnp.int32, (rows, lanes), 0)
    query_pos = lax.broadcasted_iota(jnp.int32, (rows, lanes), 1) % rows
    allowed = (key_pos <= query_pos) & (key_pos < length)
    live = (lax.broadcasted_iota(jnp.int32, (rows, HD), 0) < length).astype(BF16)
    group = groups[resp_index() * count + b]
    owners = owner_ref[pl.ds(group, 1), :]
    devices = owner_ref.shape[1]
    place = (lax.broadcasted_iota(jnp.int32, (devices, devices), 0) == owners).astype(BF16)
    own_kv = own_ref[...]
    cached = cache_ref[...]
    heads = [slice(h * HD, (h + 1) * HD) for h in range(QH)]
    key_cols = heads[:KVH]
    value_cols = heads[KVH : 2 * KVH]
    each = range(KVH)
    q = [jnp.concatenate([q_ref[:, h] for h in heads[k * PER : (k + 1) * PER]], axis=0) for k in each]
    keys = [jnp.concatenate([cached[:, at], own_kv[:, at]], axis=0) for at in key_cols]
    scores = [dot(keys[k], q[k], ((1,), (1,))) for k in each]
    do = [jnp.concatenate([do_ref[:, h] * live for h in heads[k * PER : (k + 1) * PER]], axis=0) for k in each]
    values = [jnp.concatenate([cached[:, at], own_kv[:, at]], axis=0) for at in value_cols]
    prob_grad = [dot(values[k], do[k], ((1,), (1,))) for k in each]
    low, score_grad = [], []
    for k in each:
        masked = jnp.concatenate([scores[k][:plen], jnp.where(allowed, scores[k][plen:], -1e30)], axis=0)
        expo = jnp.exp2((masked - jnp.max(masked, axis=0, keepdims=True)) * (scaling * LOG2E))
        probs = expo * (1.0 / jnp.sum(expo, axis=0, keepdims=True))
        low.append(probs.astype(BF16))
        delta = jnp.sum(low[k].astype(F32) * prob_grad[k], axis=0, keepdims=True)
        score_grad.append((probs * ((prob_grad[k] - delta) * scaling)).astype(BF16))
    grads = []
    for k in each:
        grads.append((k, 1, value_cols[k], dot(low[k], do[k], ((1,), (0,)))))
        grads.append((k, 0, key_cols[k], dot(score_grad[k], q[k], ((1,), (0,)))))
    for k in each:
        dq = dot(score_grad[k], keys[k], ((0,), (0,)))
        for g, h in enumerate(heads[k * PER : (k + 1) * PER]):
            dq_ref[:, h] = dq[g * rows : (g + 1) * rows].astype(BF16)
    for k, half, at, grad in grads:
        down_ref[:, at] = grad[plen:].astype(BF16)
        part = dot(place, grad[:plen].astype(BF16), ((1,), (0,)))
        mixed_ref[k, pl.ds(2 * b + half, devices, stride=2 * count), :] = part

    @pl.when(b == count - 1)
    def _():
        for k in range(KVH):
            send_ref[:, k * HD : (k + 1) * HD] = mixed_ref[k].astype(BF16)


def attention(queries, out_grad, resp_kv, prompt_kv, group_list, lengths, owner_map):
    count, plen, _ = prompt_kv.shape
    total = queries.shape[0]
    rows = total // count
    width = queries.shape[1]
    by_resp = lambda w: pl.BlockSpec((rows, w), lambda b, *_: (b, 0))
    return pl.pallas_call(
        attention_kernel,
        grid_spec=pltpu.PrefetchScalarGridSpec(
            num_scalar_prefetch=2,
            grid=(count,),
            in_specs=[
                by_resp(width),
                by_resp(width),
                by_resp(WIDE),
                pl.BlockSpec((None, plen, WIDE), lambda b, *_: (b, 0, 0)),
                pl.BlockSpec(owner_map.shape, lambda b, *_: (0, 0)),
            ],
            out_specs=[
                by_resp(width),
                by_resp(WIDE),
                pl.BlockSpec((2 * count * plen, WIDE // 2), lambda b, *_: (0, 0)),
            ],
            scratch_shapes=[pltpu.VMEM((KVH, 2 * count * plen, HD), F32)],
        ),
        out_shape=[
            jax.ShapeDtypeStruct((total, width), BF16),
            jax.ShapeDtypeStruct((total, WIDE), BF16),
            jax.ShapeDtypeStruct((2 * count * plen, WIDE // 2), BF16),
        ],
        cost_estimate=pl.CostEstimate(flops=10**9, bytes_accessed=6 * 10**6, transcendentals=700000),
        name="attention_backward",
    )(group_list, lengths, queries, out_grad, resp_kv, prompt_kv, owner_map)


def page_kernel(groups_ref, arrived_ref, page_ref):
    copies, prompts, _ = page_ref.shape
    rows, half = arrived_ref.shape
    ids = lax.broadcasted_iota(jnp.int32, (2 * prompts, rows), 0)
    odd = lax.broadcasted_iota(jnp.int32, (2 * prompts, rows), 1) % 2
    select = (ids == groups_ref[...] + prompts * odd).astype(BF16)
    page = dot(select, arrived_ref[...], ((1,), (0,))).astype(BF16)
    for copy in range(copies):
        page_ref[copy, :, :half] = page[:prompts]
        page_ref[copy, :, half:] = page[prompts:]


def natural_order(transposed):
    span = 2 * LANES
    held = lax.broadcasted_iota(jnp.int32, (span, span), 1 if transposed else 0)
    model = lax.broadcasted_iota(jnp.int32, (span, span), 0 if transposed else 1)
    rows = 32
    core, rest = held // LANES, held % LANES
    return (model == rest // rows * (2 * rows) + core * rows + rest % rows).astype(BF16)


def collect_kernel(*refs):
    out_ref, pieces = refs[-1], refs[:-1]
    block, at = out_ref.shape[1], 0
    for ref in pieces:
        for start in range(0, ref.shape[0], block):
            out_ref[at] = ref[start : start + block]
            at += 1


def project_kernel(pages_ref, own_ref, sibling_ref, near_ref, far_ref, gain_ref, out_ref, gain_rows, weight_ref):
    span = 2 * LANES
    gain = gain_ref[...].astype(F32)
    gain = jnp.concatenate([gain[:, start : start + span] for start in range(0, gain.shape[1], span)], axis=0)
    gain_rows[...] = dot(gain.astype(BF16), natural_order(True), ((1,), (0,)))
    cores, rows, block, _ = weight_ref.shape
    core, row = lax.axis_index("core"), lax.axis_index("y")
    other = 1 - core
    weight_ref[core, row] = own_ref[...]
    weight_ref[other, row] = sibling_ref[...]
    for j in range(1, rows // 2):
        below = lax.rem(row + rows - j, rows)
        above = lax.rem(row + j, rows)
        near = jnp.where(core == 0, below, above)
        far = jnp.where(core == 0, above, below)
        weight_ref[core, near] = near_ref[2 * j - 2]
        weight_ref[other, near] = near_ref[2 * j - 1]
        weight_ref[other, far] = far_ref[2 * j - 2]
        weight_ref[core, far] = far_ref[2 * j - 1]
    middle = lax.rem(row + rows // 2, rows)
    weight_ref[core, middle] = near_ref[rows - 2]
    weight_ref[other, middle] = far_ref[rows - 2]
    cols = rows * block
    pairs = cols // LANES
    scales = [gain_rows[pl.ds(lax.axis_index("z") * pairs + pair, 1), :] for pair in range(pairs)]
    for c in range(cores):
        normed = dot(pages_ref[...], weight_ref[c].reshape(cols, WIDE), ((1,), (1,)))
        for pair in range(pairs):
            at = slice(pair * LANES, (pair + 1) * LANES)
            start = c * cols + pair * LANES
            out_ref[:, start : start + LANES] = (normed[:, at] * scales[pair][:, c * LANES : (c + 1) * LANES]).astype(BF16)


def term_kernel(scaled_ref, hidden_ref, *refs):
    got, (out_ref, term_ref, layers_ref) = refs[:-3], refs[-3:]
    blocks, rows, cols = scaled_ref.shape
    sections, step, width = layers_ref.shape
    here = lax.axis_index("section")
    layers_ref[here] = hidden_ref[here].astype(F32)
    for k, ref in enumerate(got, 1):
        layers_ref[lax.rem(here + sections - k, sections)] = ref[...].astype(F32)
    span = 2 * LANES
    pairs = cols // span
    mixed = []
    for block in range(blocks):
        for pair in range(pairs):
            low, high = pair * LANES, (pairs + pair) * LANES
            mixed.append(
                jnp.concatenate([scaled_ref[block, :, low : low + LANES], scaled_ref[block, :, high : high + LANES]], axis=1)
            )
    scaled = dot(jnp.concatenate(mixed, axis=0), natural_order(False), ((1,), (0,)))
    squares = jnp.zeros((rows, span), F32)
    cross = jnp.zeros((rows, span), F32)
    for n in range(len(mixed)):
        at = slice(n * span, (n + 1) * span)
        part = scaled[n * rows : (n + 1) * rows]
        term_ref[:, at] = part
        hidden = layers_ref[:, :, at].reshape(rows, span)
        squares += hidden * hidden
        cross += hidden * part
    inverse = lax.rsqrt(jnp.sum(squares, axis=-1, keepdims=True) / width + 1e-06)
    back = inverse**3 * (jnp.sum(cross, axis=-1, keepdims=True) / width)
    chunk = 4 * LANES
    for start in range(0, width, chunk):
        at = slice(start, start + chunk)
        term = inverse * term_ref[:, at] - layers_ref[:, :, at].reshape(rows, chunk) * back
        sums = [term[(sections - 1) * step :]]
        for s in reversed(range(sections - 1)):
            sums.insert(0, sums[0] + term[s * step : (s + 1) * step])
        out_ref[:, at] = jnp.concatenate(sums, axis=0).astype(BF16)


def finish(pages, weights, hidden, norm_gain, upper_grad):
    prompt_count, width = upper_grad.shape
    sections, quarter, _ = hidden[0].shape
    members = pages.shape[0]
    scaled = pl.pallas_call(
        project_kernel,
        out_shape=jax.ShapeDtypeStruct((members * prompt_count, width // members), BF16),
        scratch_shapes=[
            pltpu.VMEM((width // (2 * LANES), 2 * LANES), F32),
            pltpu.VMEM((2, lax.axis_size("y")) + weights[0].shape, BF16),
        ],
        compiler_params=SMALL,
        cost_estimate=pl.CostEstimate(flops=3 * 10**8, bytes_accessed=2 * 10**6, transcendentals=0),
        name="projection",
    )(pages.reshape(-1, WIDE), *weights, norm_gain)
    scaled = scaled.reshape(members * sections, quarter, -1)
    scaled = lax.all_to_all(scaled, ("z", "section"), split_axis=0, concat_axis=0, tiled=True)
    sums = pl.pallas_call(
        term_kernel,
        out_shape=jax.ShapeDtypeStruct((prompt_count, width), BF16),
        scratch_shapes=[pltpu.VMEM((prompt_count, width), F32), pltpu.VMEM((sections, quarter, width), F32)],
        compiler_params=SMALL,
        cost_estimate=pl.CostEstimate(flops=10**8, bytes_accessed=10**6, transcendentals=0),
        name="norm_terms",
    )(scaled.reshape(members, prompt_count, -1), *hidden)
    sums = lax.all_to_all(sums.reshape(sections, quarter, width), "section", split_axis=0, concat_axis=0, tiled=True)
    return (upper_grad.astype(F32) + sums.reshape(prompt_count, width).astype(F32)).astype(BF16)


def swap(piece):
    return lax.ppermute(piece, "core", [(0, 1), (1, 0)])


def turn(piece, axis, k):
    size = lax.axis_size(axis)
    return lax.ppermute(piece, axis, [(i, (i + k) % size) for i in range(size)])


def part_ways(piece, j):
    rows = lax.axis_size("y")
    pairs = [(2 * y + c, (y + (j if c == 0 else rows - j)) % rows * 2 + c) for y in range(rows) for c in range(2)]
    return lax.ppermute(piece, ("y", "core"), pairs)


def hand_over(hidden, k):
    size, here = hidden.shape[0], lax.axis_index("section")
    return turn(lax.dynamic_index_in_dim(hidden, lax.rem(here + k, size), keepdims=False), "section", k)


def gather_rows(weight, both):
    rows = lax.axis_size("y")
    pieces = [part_ways(both, j) for j in range(1, rows // 2)] + [turn(weight, "y", rows // 2)]
    return pl.pallas_call(
        collect_kernel,
        out_shape=jax.ShapeDtypeStruct((rows - 1,) + weight.shape, BF16),
        compiler_params=SMALL,
        cost_estimate=pl.CostEstimate(flops=0, bytes_accessed=10**6, transcendentals=0),
        name="weight_rows",
    )(*pieces)


def body(queries, out_grad, resp_kv, prompt_kv, prompt_hidden, norm_gain, kv_weight, upper_grad, group_list, lengths, owner_map):
    prompt_count, devices = owner_map.shape
    sections = lax.axis_size("section")
    width = prompt_hidden.shape[-1]
    query_out, own_out, outgoing = attention(
        queries[0], out_grad[0], resp_kv[0], prompt_kv[0], group_list, lengths, owner_map
    )
    hidden = prompt_hidden[0].reshape(sections, prompt_count // sections, width)
    outgoing, weight, hidden = lax.optimization_barrier((outgoing, kv_weight[0], hidden))
    outgoing = outgoing.reshape(devices, -1, WIDE // 2)
    incoming = lax.all_to_all(outgoing, RESP_AXES, split_axis=0, concat_axis=0, tiled=True)
    sibling = swap(weight)
    both = jnp.concatenate([weight, sibling], axis=0)
    layers = [hidden] + [hand_over(hidden, k) for k in range(1, sections)]
    incoming, weight, sibling, both, layers = lax.optimization_barrier((incoming, weight, sibling, both, layers))
    pages = pl.pallas_call(
        page_kernel,
        out_shape=jax.ShapeDtypeStruct((lax.axis_size("z"), prompt_count, WIDE), BF16),
        compiler_params=SMALL,
        cost_estimate=pl.CostEstimate(flops=10**8, bytes_accessed=10**6, transcendentals=0),
        name="page_sum",
    )(jnp.repeat(group_list, 2)[None, :], incoming.reshape(-1, WIDE // 2))
    pages = lax.all_to_all(pages, "z", split_axis=0, concat_axis=0, tiled=True)
    near = gather_rows(weight, both)
    far = swap(near)
    prompt_out = finish(pages, [weight, sibling, near, far], layers, norm_gain, upper_grad)
    return (query_out[None], own_out[None], prompt_out[None])


def solution(mesh):
    wide = jax.sharding.Mesh(mesh.devices.reshape(8, 8, 2, mesh.shape["section"]), RESP_AXES + ("section",))
    in_specs = (
        P("section", RESP_AXES, None),
        P("section", RESP_AXES, None),
        P("section", RESP_AXES, None),
        P("section", RESP_AXES, None, None),
        P("section", RESP_AXES, None),
        P("section", None),
        P("section", RESP_AXES, None),
        P(RESP_AXES, None),
        P(),
        P(RESP_AXES),
        P(),
    )
    out_specs = (P("section", RESP_AXES, None),) * 3
    return jax.shard_map(body, mesh=wide, in_specs=in_specs, out_specs=out_specs, check_vma=False)
```

```python
import functools

import jax
import jax.numpy as jnp
from jax import lax
from jax.experimental import pallas as pl
from jax.experimental.pallas import tpu as pltpu
from jax.sharding import PartitionSpec as P

QH = 32
KVH = 4
HD = 128
PER = QH // KVH
RESP_DEV = 4
WIDE = 2 * KVH * HD
LOG2E = 1.4426950408889634
SMALL = pltpu.CompilerParams(vmem_limit_bytes=16 * 1024 * 1024)
F32 = jnp.float32
BF16 = jnp.bfloat16


def dot(a, b, dims):
    return lax.dot_general(a, b, (dims, ((), ())), preferred_element_type=F32)


RESP_AXES = ("z", "y", "core")
LANES = 128


def resp_index():
    index = 0
    for axis in RESP_AXES:
        index = index * lax.axis_size(axis) + lax.axis_index(axis)
    return index


def attention_kernel(groups, lengths, q_ref, do_ref, own_ref, cache_ref, owner_ref, dq_ref, down_ref, send_ref, mixed_ref):
    b = pl.program_id(0)
    count = RESP_DEV
    length = lengths[b]
    rows = q_ref.shape[0]
    plen = cache_ref.shape[0]
    scaling = HD ** (-0.5)
    lanes = PER * rows
    key_pos = lax.broadcasted_iota(jnp.int32, (rows, lanes), 0)
    query_pos = lax.broadcasted_iota(jnp.int32, (rows, lanes), 1) % rows
    allowed = (key_pos <= query_pos) & (key_pos < length)
    live = (lax.broadcasted_iota(jnp.int32, (rows, HD), 0) < length).astype(BF16)
    group = groups[resp_index() * count + b]
    owners = owner_ref[pl.ds(group, 1), :]
    devices = owner_ref.shape[1]
    place = (lax.broadcasted_iota(jnp.int32, (devices, devices), 0) == owners).astype(BF16)
    own_kv = own_ref[...]
    cached = cache_ref[...]
    heads = [slice(h * HD, (h + 1) * HD) for h in range(QH)]
    key_cols = heads[:KVH]
    value_cols = heads[KVH : 2 * KVH]
    each = range(KVH)
    q = [jnp.concatenate([q_ref[:, h] for h in heads[k * PER : (k + 1) * PER]], axis=0) for k in each]
    keys = [jnp.concatenate([cached[:, at], own_kv[:, at]], axis=0) for at in key_cols]
    scores = [dot(keys[k], q[k], ((1,), (1,))) for k in each]
    do = [jnp.concatenate([do_ref[:, h] * live for h in heads[k * PER : (k + 1) * PER]], axis=0) for k in each]
    values = [jnp.concatenate([cached[:, at], own_kv[:, at]], axis=0) for at in value_cols]
    prob_grad = [dot(values[k], do[k], ((1,), (1,))) for k in each]
    low, score_grad = [], []
    for k in each:
        masked = jnp.concatenate([scores[k][:plen], jnp.where(allowed, scores[k][plen:], -1e30)], axis=0)
        expo = jnp.exp2((masked - jnp.max(masked, axis=0, keepdims=True)) * (scaling * LOG2E))
        probs = expo * (1.0 / jnp.sum(expo, axis=0, keepdims=True))
        low.append(probs.astype(BF16))
        delta = jnp.sum(low[k].astype(F32) * prob_grad[k], axis=0, keepdims=True)
        score_grad.append((probs * ((prob_grad[k] - delta) * scaling)).astype(BF16))
    grads = []
    for k in each:
        grads.append((k, 1, value_cols[k], dot(low[k], do[k], ((1,), (0,)))))
        grads.append((k, 0, key_cols[k], dot(score_grad[k], q[k], ((1,), (0,)))))
    for k in each:
        dq = dot(score_grad[k], keys[k], ((0,), (0,)))
        for g, h in enumerate(heads[k * PER : (k + 1) * PER]):
            dq_ref[:, h] = dq[g * rows : (g + 1) * rows].astype(BF16)
    for k, half, at, grad in grads:
        down_ref[:, at] = grad[plen:].astype(BF16)
        part = dot(place, grad[:plen].astype(BF16), ((1,), (0,)))
        mixed_ref[k, pl.ds(2 * b + half, devices, stride=2 * count), :] = part

    @pl.when(b == count - 1)
    def _():
        for k in range(KVH):
            send_ref[:, k * HD : (k + 1) * HD] = mixed_ref[k].astype(BF16)


def attention(queries, out_grad, resp_kv, prompt_kv, group_list, lengths, owner_map):
    count, plen, _ = prompt_kv.shape
    total = queries.shape[0]
    rows = total // count
    width = queries.shape[1]
    by_resp = lambda w: pl.BlockSpec((rows, w), lambda b, *_: (b, 0))
    return pl.pallas_call(
        attention_kernel,
        grid_spec=pltpu.PrefetchScalarGridSpec(
            num_scalar_prefetch=2,
            grid=(count,),
            in_specs=[
                by_resp(width),
                by_resp(width),
                by_resp(WIDE),
                pl.BlockSpec((None, plen, WIDE), lambda b, *_: (b, 0, 0)),
                pl.BlockSpec(owner_map.shape, lambda b, *_: (0, 0)),
            ],
            out_specs=[
                by_resp(width),
                by_resp(WIDE),
                pl.BlockSpec((2 * count * plen, WIDE // 2), lambda b, *_: (0, 0)),
            ],
            scratch_shapes=[pltpu.VMEM((KVH, 2 * count * plen, HD), F32)],
        ),
        out_shape=[
            jax.ShapeDtypeStruct((total, width), BF16),
            jax.ShapeDtypeStruct((total, WIDE), BF16),
            jax.ShapeDtypeStruct((2 * count * plen, WIDE // 2), BF16),
        ],
        cost_estimate=pl.CostEstimate(flops=10**9, bytes_accessed=6 * 10**6, transcendentals=700000),
        name="attention_backward",
    )(group_list, lengths, queries, out_grad, resp_kv, prompt_kv, owner_map)


def page_kernel(groups_ref, arrived_ref, page_ref):
    copies, prompts, _ = page_ref.shape
    rows, half = arrived_ref.shape
    ids = lax.broadcasted_iota(jnp.int32, (2 * prompts, rows), 0)
    odd = lax.broadcasted_iota(jnp.int32, (2 * prompts, rows), 1) % 2
    select = (ids == groups_ref[...] + prompts * odd).astype(BF16)
    page = dot(select, arrived_ref[...], ((1,), (0,))).astype(BF16)
    for copy in range(copies):
        page_ref[copy, :, :half] = page[:prompts]
        page_ref[copy, :, half:] = page[prompts:]


def natural_order(transposed):
    span = 2 * LANES
    held = lax.broadcasted_iota(jnp.int32, (span, span), 1 if transposed else 0)
    model = lax.broadcasted_iota(jnp.int32, (span, span), 0 if transposed else 1)
    rows = 32
    core, rest = held // LANES, held % LANES
    return (model == rest // rows * (2 * rows) + core * rows + rest % rows).astype(BF16)


def collect_kernel(*refs):
    out_ref, pieces = refs[-1], refs[:-1]
    block, at = out_ref.shape[1], 0
    for ref in pieces:
        for start in range(0, ref.shape[0], block):
            out_ref[at] = ref[start : start + block]
            at += 1


def project_kernel(pages_ref, own_ref, sibling_ref, near_ref, far_ref, gain_ref, out_ref, gain_rows, weight_ref):
    span = 2 * LANES
    gain = gain_ref[...].astype(F32)
    gain = jnp.concatenate([gain[:, start : start + span] for start in range(0, gain.shape[1], span)], axis=0)
    gain_rows[...] = dot(gain.astype(BF16), natural_order(True), ((1,), (0,)))
    cores, rows, block, _ = weight_ref.shape
    core, row = lax.axis_index("core"), lax.axis_index("y")
    other = 1 - core
    weight_ref[core, row] = own_ref[...]
    weight_ref[other, row] = sibling_ref[...]
    for j in range(1, rows // 2):
        below = lax.rem(row + rows - j, rows)
        above = lax.rem(row + j, rows)
        near = jnp.where(core == 0, below, above)
        far = jnp.where(core == 0, above, below)
        weight_ref[core, near] = near_ref[2 * j - 2]
        weight_ref[other, near] = near_ref[2 * j - 1]
        weight_ref[other, far] = far_ref[2 * j - 2]
        weight_ref[core, far] = far_ref[2 * j - 1]
    middle = lax.rem(row + rows // 2, rows)
    weight_ref[core, middle] = near_ref[rows - 2]
    weight_ref[other, middle] = far_ref[rows - 2]
    cols = rows * block
    pairs = cols // LANES
    scales = [gain_rows[pl.ds(lax.axis_index("z") * pairs + pair, 1), :] for pair in range(pairs)]
    for c in range(cores):
        normed = dot(pages_ref[...], weight_ref[c].reshape(cols, WIDE), ((1,), (1,)))
        for pair in range(pairs):
            at = slice(pair * LANES, (pair + 1) * LANES)
            start = c * cols + pair * LANES
            out_ref[:, start : start + LANES] = (normed[:, at] * scales[pair][:, c * LANES : (c + 1) * LANES]).astype(BF16)


def term_kernel(scaled_ref, hidden_ref, *refs):
    got, (out_ref, term_ref, layers_ref) = refs[:-3], refs[-3:]
    blocks, rows, cols = scaled_ref.shape
    sections, step, width = layers_ref.shape
    here = lax.axis_index("section")
    layers_ref[here] = hidden_ref[here].astype(F32)
    for k, ref in enumerate(got, 1):
        layers_ref[lax.rem(here + sections - k, sections)] = ref[...].astype(F32)
    span = 2 * LANES
    pairs = cols // span
    mixed = []
    for block in range(blocks):
        for pair in range(pairs):
            low, high = pair * LANES, (pairs + pair) * LANES
            mixed.append(
                jnp.concatenate([scaled_ref[block, :, low : low + LANES], scaled_ref[block, :, high : high + LANES]], axis=1)
            )
    scaled = dot(jnp.concatenate(mixed, axis=0), natural_order(False), ((1,), (0,)))
    squares = jnp.zeros((rows, span), F32)
    cross = jnp.zeros((rows, span), F32)
    for n in range(len(mixed)):
        at = slice(n * span, (n + 1) * span)
        part = scaled[n * rows : (n + 1) * rows]
        term_ref[:, at] = part
        hidden = layers_ref[:, :, at].reshape(rows, span)
        squares += hidden * hidden
        cross += hidden * part
    inverse = lax.rsqrt(jnp.sum(squares, axis=-1, keepdims=True) / width + 1e-06)
    back = inverse**3 * (jnp.sum(cross, axis=-1, keepdims=True) / width)
    chunk = 4 * LANES
    for start in range(0, width, chunk):
        at = slice(start, start + chunk)
        term = inverse * term_ref[:, at] - layers_ref[:, :, at].reshape(rows, chunk) * back
        sums = [term[(sections - 1) * step :]]
        for s in reversed(range(sections - 1)):
            sums.insert(0, sums[0] + term[s * step : (s + 1) * step])
        out_ref[:, at] = jnp.concatenate(sums, axis=0).astype(BF16)


def finish(pages, weights, hidden, norm_gain, upper_grad):
    prompt_count, width = upper_grad.shape
    sections, quarter, _ = hidden[0].shape
    members = pages.shape[0]
    scaled = pl.pallas_call(
        project_kernel,
        out_shape=jax.ShapeDtypeStruct((members * prompt_count, width // members), BF16),
        scratch_shapes=[
            pltpu.VMEM((width // (2 * LANES), 2 * LANES), F32),
            pltpu.VMEM((2, lax.axis_size("y")) + weights[0].shape, BF16),
        ],
        compiler_params=SMALL,
        cost_estimate=pl.CostEstimate(flops=3 * 10**8, bytes_accessed=2 * 10**6, transcendentals=0),
        name="projection",
    )(pages.reshape(-1, WIDE), *weights, norm_gain)
    scaled = scaled.reshape(members * sections, quarter, -1)
    scaled = lax.all_to_all(scaled, ("z", "section"), split_axis=0, concat_axis=0, tiled=True)
    sums = pl.pallas_call(
        term_kernel,
        out_shape=jax.ShapeDtypeStruct((prompt_count, width), BF16),
        scratch_shapes=[pltpu.VMEM((prompt_count, width), F32), pltpu.VMEM((sections, quarter, width), F32)],
        compiler_params=SMALL,
        cost_estimate=pl.CostEstimate(flops=10**8, bytes_accessed=10**6, transcendentals=0),
        name="norm_terms",
    )(scaled.reshape(members, prompt_count, -1), *hidden)
    sums = lax.all_to_all(sums.reshape(sections, quarter, width), "section", split_axis=0, concat_axis=0, tiled=True)
    return (upper_grad.astype(F32) + sums.reshape(prompt_count, width).astype(F32)).astype(BF16)


def swap(piece):
    return lax.ppermute(piece, "core", [(0, 1), (1, 0)])


def turn(piece, axis, k):
    size = lax.axis_size(axis)
    return lax.ppermute(piece, axis, [(i, (i + k) % size) for i in range(size)])


def part_ways(piece, j):
    rows = lax.axis_size("y")
    pairs = [(2 * y + c, (y + (j if c == 0 else rows - j)) % rows * 2 + c) for y in range(rows) for c in range(2)]
    return lax.ppermute(piece, ("y", "core"), pairs)


def hand_over(hidden, k):
    size, here = hidden.shape[0], lax.axis_index("section")
    return turn(lax.dynamic_index_in_dim(hidden, lax.rem(here + k, size), keepdims=False), "section", k)


def collect(pieces, block):
    count = sum(piece.shape[0] for piece in pieces) // block
    return pl.pallas_call(
        collect_kernel,
        out_shape=jax.ShapeDtypeStruct((count, block, WIDE), BF16),
        compiler_params=SMALL,
        cost_estimate=pl.CostEstimate(flops=0, bytes_accessed=10**6, transcendentals=0),
        name="weight_rows",
    )(*pieces)


def body(queries, out_grad, resp_kv, prompt_kv, prompt_hidden, norm_gain, kv_weight, upper_grad, group_list, lengths, owner_map):
    prompt_count, devices = owner_map.shape
    sections = lax.axis_size("section")
    width = prompt_hidden.shape[-1]
    middle = turn(kv_weight[0], "y", lax.axis_size("y") // 2)
    query_out, own_out, outgoing = attention(
        queries[0], out_grad[0], resp_kv[0], prompt_kv[0], group_list, lengths, owner_map
    )
    hidden = prompt_hidden[0].reshape(sections, prompt_count // sections, width)
    outgoing, weight, hidden, middle = lax.optimization_barrier((outgoing, kv_weight[0], hidden, middle))
    outgoing = outgoing.reshape(devices, -1, WIDE // 2)
    incoming = lax.all_to_all(outgoing, RESP_AXES, split_axis=0, concat_axis=0, tiled=True)
    layers = [hidden, hand_over(hidden, 1)]
    sibling = swap(weight)
    both, hidden = lax.optimization_barrier((jnp.concatenate([weight, sibling], axis=0), hidden))
    near = [part_ways(both, 1), part_ways(both, 2)]
    layers += [hand_over(hidden, k) for k in range(2, sections)]
    incoming, both, near, layers = lax.optimization_barrier((incoming, both, near, layers))
    pages = pl.pallas_call(
        page_kernel,
        out_shape=jax.ShapeDtypeStruct((lax.axis_size("z"), prompt_count, WIDE), BF16),
        compiler_params=SMALL,
        cost_estimate=pl.CostEstimate(flops=10**8, bytes_accessed=10**6, transcendentals=0),
        name="page_sum",
    )(jnp.repeat(group_list, 2)[None, :], incoming.reshape(-1, WIDE // 2))
    pages = lax.all_to_all(pages, "z", split_axis=0, concat_axis=0, tiled=True)
    near = collect(near + [part_ways(both, 3), middle], weight.shape[0])
    far = swap(near)
    prompt_out = finish(pages, [weight, sibling, near, far], layers, norm_gain, upper_grad)
    return (query_out[None], own_out[None], prompt_out[None])


def solution(mesh):
    wide = jax.sharding.Mesh(mesh.devices.reshape(8, 8, 2, mesh.shape["section"]), RESP_AXES + ("section",))
    in_specs = (
        P("section", RESP_AXES, None),
        P("section", RESP_AXES, None),
        P("section", RESP_AXES, None),
        P("section", RESP_AXES, None, None),
        P("section", RESP_AXES, None),
        P("section", None),
        P("section", RESP_AXES, None),
        P(RESP_AXES, None),
        P(),
        P(RESP_AXES),
        P(),
    )
    out_specs = (P("section", RESP_AXES, None),) * 3
    return jax.shard_map(body, mesh=wide, in_specs=in_specs, out_specs=out_specs, check_vma=False)
```

```python
import functools

import jax
import jax.numpy as jnp
from jax import lax
from jax.experimental import pallas as pl
from jax.experimental.pallas import tpu as pltpu
from jax.sharding import PartitionSpec as P

QH = 32
KVH = 4
HD = 128
PER = QH // KVH
RESP_DEV = 4
WIDE = 2 * KVH * HD
LOG2E = 1.4426950408889634
SMALL = pltpu.CompilerParams(vmem_limit_bytes=16 * 1024 * 1024)
F32 = jnp.float32
BF16 = jnp.bfloat16


def dot(a, b, dims):
    return lax.dot_general(a, b, (dims, ((), ())), preferred_element_type=F32)


RESP_AXES = ("z", "y", "core")
LANES = 128


def resp_index():
    index = 0
    for axis in RESP_AXES:
        index = index * lax.axis_size(axis) + lax.axis_index(axis)
    return index


def attention_kernel(groups, lengths, q_ref, do_ref, own_ref, cache_ref, owner_ref, grad_ref, down_ref, send_ref, mixed_ref):
    b = pl.program_id(0)
    count = RESP_DEV
    length = lengths[b]
    rows = q_ref.shape[0]
    plen = cache_ref.shape[0]
    scaling = HD ** (-0.5)
    lanes = PER * rows
    key_pos = lax.broadcasted_iota(jnp.int32, (rows, lanes), 0)
    query_pos = lax.broadcasted_iota(jnp.int32, (rows, lanes), 1) % rows
    allowed = (key_pos <= query_pos) & (key_pos < length)
    live = (lax.broadcasted_iota(jnp.int32, (rows, HD), 0) < length).astype(BF16)
    group = groups[resp_index() * count + b]
    owners = owner_ref[pl.ds(group, 1), :]
    devices = owner_ref.shape[1]
    place = (lax.broadcasted_iota(jnp.int32, (devices, devices), 0) == owners).astype(BF16)
    own_kv = own_ref[...]
    cached = cache_ref[...]
    heads = [slice(h * HD, (h + 1) * HD) for h in range(QH)]
    key_cols = heads[:KVH]
    value_cols = heads[KVH : 2 * KVH]
    each = range(KVH)
    q = [jnp.concatenate([q_ref[:, h] for h in heads[k * PER : (k + 1) * PER]], axis=0) for k in each]
    keys = [jnp.concatenate([cached[:, at], own_kv[:, at]], axis=0) for at in key_cols]
    scores = [dot(keys[k], q[k], ((1,), (1,))) for k in each]
    do = [jnp.concatenate([do_ref[:, h] * live for h in heads[k * PER : (k + 1) * PER]], axis=0) for k in each]
    values = [jnp.concatenate([cached[:, at], own_kv[:, at]], axis=0) for at in value_cols]
    prob_grad = [dot(values[k], do[k], ((1,), (1,))) for k in each]
    low, score_grad = [], []
    for k in each:
        masked = jnp.concatenate([scores[k][:plen], jnp.where(allowed, scores[k][plen:], -1e30)], axis=0)
        expo = jnp.exp2((masked - jnp.max(masked, axis=0, keepdims=True)) * (scaling * LOG2E))
        probs = expo * (1.0 / jnp.sum(expo, axis=0, keepdims=True))
        low.append(probs.astype(BF16))
        delta = jnp.sum(low[k].astype(F32) * prob_grad[k], axis=0, keepdims=True)
        score_grad.append((probs * ((prob_grad[k] - delta) * scaling)).astype(BF16))
    grads = []
    for k in each:
        grads.append((k, 1, value_cols[k], dot(low[k], do[k], ((1,), (0,)))))
        grads.append((k, 0, key_cols[k], dot(score_grad[k], q[k], ((1,), (0,)))))
    for k in each:
        grad_ref[k] = score_grad[k]
    for k, half, at, grad in grads:
        down_ref[:, at] = grad[plen:].astype(BF16)
        part = dot(place, grad[:plen].astype(BF16), ((1,), (0,)))
        mixed_ref[k, pl.ds(2 * b + half, devices, stride=2 * count), :] = part

    @pl.when(b == count - 1)
    def _():
        for k in range(KVH):
            send_ref[:, k * HD : (k + 1) * HD] = mixed_ref[k].astype(BF16)


def attention(queries, out_grad, resp_kv, prompt_kv, group_list, lengths, owner_map):
    count, plen, _ = prompt_kv.shape
    total = queries.shape[0]
    rows = total // count
    width = queries.shape[1]
    keys, lanes = plen + rows, PER * rows
    by_resp = lambda w: pl.BlockSpec((rows, w), lambda b, *_: (b, 0))
    return pl.pallas_call(
        attention_kernel,
        grid_spec=pltpu.PrefetchScalarGridSpec(
            num_scalar_prefetch=2,
            grid=(count,),
            in_specs=[
                by_resp(width),
                by_resp(width),
                by_resp(WIDE),
                pl.BlockSpec((None, plen, WIDE), lambda b, *_: (b, 0, 0)),
                pl.BlockSpec(owner_map.shape, lambda b, *_: (0, 0)),
            ],
            out_specs=[
                pl.BlockSpec((KVH, keys, lanes), lambda b, *_: (b, 0, 0)),
                by_resp(WIDE),
                pl.BlockSpec((2 * count * plen, WIDE // 2), lambda b, *_: (0, 0)),
            ],
            scratch_shapes=[pltpu.VMEM((KVH, 2 * count * plen, HD), F32)],
        ),
        out_shape=[
            jax.ShapeDtypeStruct((count * KVH, keys, lanes), BF16),
            jax.ShapeDtypeStruct((total, WIDE), BF16),
            jax.ShapeDtypeStruct((2 * count * plen, WIDE // 2), BF16),
        ],
        cost_estimate=pl.CostEstimate(flops=10**9, bytes_accessed=6 * 10**6, transcendentals=700000),
        name="attention_backward",
    )(group_list, lengths, queries, out_grad, resp_kv, prompt_kv, owner_map)


def query_kernel(grad_ref, own_ref, cache_ref, dq_ref):
    rows = dq_ref.shape[0]
    for k in range(KVH):
        at = slice(k * HD, (k + 1) * HD)
        keys = jnp.concatenate([cache_ref[:, at], own_ref[:, at]], axis=0)
        dq = dot(grad_ref[k], keys, ((0,), (0,)))
        for g in range(PER):
            h = k * PER + g
            dq_ref[:, h * HD : (h + 1) * HD] = dq[g * rows : (g + 1) * rows].astype(BF16)


def query_gradient(score_grad, resp_kv, prompt_kv):
    count, plen, _ = prompt_kv.shape
    total = resp_kv.shape[0]
    rows = total // count
    half = KVH * HD
    return pl.pallas_call(
        query_kernel,
        grid=(count,),
        in_specs=[
            pl.BlockSpec((KVH,) + score_grad.shape[1:], lambda b: (b, 0, 0)),
            pl.BlockSpec((rows, half), lambda b: (b, 0)),
            pl.BlockSpec((None, plen, half), lambda b: (b, 0, 0)),
        ],
        out_specs=pl.BlockSpec((rows, QH * HD), lambda b: (b, 0)),
        out_shape=jax.ShapeDtypeStruct((total, QH * HD), BF16),
        cost_estimate=pl.CostEstimate(flops=2 * 10**8, bytes_accessed=4 * 10**6, transcendentals=0),
        name="query_gradient",
    )(score_grad, resp_kv, prompt_kv)


def page_kernel(groups_ref, arrived_ref, page_ref):
    copies, prompts, _ = page_ref.shape
    rows, half = arrived_ref.shape
    ids = lax.broadcasted_iota(jnp.int32, (2 * prompts, rows), 0)
    odd = lax.broadcasted_iota(jnp.int32, (2 * prompts, rows), 1) % 2
    select = (ids == groups_ref[...] + prompts * odd).astype(BF16)
    page = dot(select, arrived_ref[...], ((1,), (0,))).astype(BF16)
    for copy in range(copies):
        page_ref[copy, :, :half] = page[:prompts]
        page_ref[copy, :, half:] = page[prompts:]


def natural_order(transposed):
    span = 2 * LANES
    held = lax.broadcasted_iota(jnp.int32, (span, span), 1 if transposed else 0)
    model = lax.broadcasted_iota(jnp.int32, (span, span), 0 if transposed else 1)
    rows = 32
    core, rest = held // LANES, held % LANES
    return (model == rest // rows * (2 * rows) + core * rows + rest % rows).astype(BF16)


def collect_kernel(*refs):
    out_ref, pieces = refs[-1], refs[:-1]
    block, at = out_ref.shape[1], 0
    for ref in pieces:
        for start in range(0, ref.shape[0], block):
            out_ref[at] = ref[start : start + block]
            at += 1


def project_kernel(pages_ref, own_ref, sibling_ref, near_ref, far_ref, gain_ref, out_ref, gain_rows, weight_ref):
    span = 2 * LANES
    gain = gain_ref[...].astype(F32)
    gain = jnp.concatenate([gain[:, start : start + span] for start in range(0, gain.shape[1], span)], axis=0)
    gain_rows[...] = dot(gain.astype(BF16), natural_order(True), ((1,), (0,)))
    cores, rows, block, _ = weight_ref.shape
    core, row = lax.axis_index("core"), lax.axis_index("y")
    other = 1 - core
    weight_ref[core, row] = own_ref[...]
    weight_ref[other, row] = sibling_ref[...]
    for j in range(1, rows // 2):
        below = lax.rem(row + rows - j, rows)
        above = lax.rem(row + j, rows)
        near = jnp.where(core == 0, below, above)
        far = jnp.where(core == 0, above, below)
        weight_ref[core, near] = near_ref[2 * j - 2]
        weight_ref[other, near] = near_ref[2 * j - 1]
        weight_ref[other, far] = far_ref[2 * j - 2]
        weight_ref[core, far] = far_ref[2 * j - 1]
    middle = lax.rem(row + rows // 2, rows)
    weight_ref[core, middle] = near_ref[rows - 2]
    weight_ref[other, middle] = far_ref[rows - 2]
    cols = rows * block
    pairs = cols // LANES
    scales = [gain_rows[pl.ds(lax.axis_index("z") * pairs + pair, 1), :] for pair in range(pairs)]
    for c in range(cores):
        normed = dot(pages_ref[...], weight_ref[c].reshape(cols, WIDE), ((1,), (1,)))
        for pair in range(pairs):
            at = slice(pair * LANES, (pair + 1) * LANES)
            start = c * cols + pair * LANES
            out_ref[:, start : start + LANES] = (normed[:, at] * scales[pair][:, c * LANES : (c + 1) * LANES]).astype(BF16)


def term_kernel(scaled_ref, hidden_ref, *refs):
    got, (out_ref, term_ref, layers_ref) = refs[:-3], refs[-3:]
    blocks, rows, cols = scaled_ref.shape
    sections, step, width = layers_ref.shape
    here = lax.axis_index("section")
    layers_ref[here] = hidden_ref[here].astype(F32)
    for k, ref in enumerate(got, 1):
        layers_ref[lax.rem(here + sections - k, sections)] = ref[...].astype(F32)
    span = 2 * LANES
    pairs = cols // span
    mixed = []
    for block in range(blocks):
        for pair in range(pairs):
            low, high = pair * LANES, (pairs + pair) * LANES
            mixed.append(
                jnp.concatenate([scaled_ref[block, :, low : low + LANES], scaled_ref[block, :, high : high + LANES]], axis=1)
            )
    scaled = dot(jnp.concatenate(mixed, axis=0), natural_order(False), ((1,), (0,)))
    squares = jnp.zeros((rows, span), F32)
    cross = jnp.zeros((rows, span), F32)
    for n in range(len(mixed)):
        at = slice(n * span, (n + 1) * span)
        part = scaled[n * rows : (n + 1) * rows]
        term_ref[:, at] = part
        hidden = layers_ref[:, :, at].reshape(rows, span)
        squares += hidden * hidden
        cross += hidden * part
    inverse = lax.rsqrt(jnp.sum(squares, axis=-1, keepdims=True) / width + 1e-06)
    back = inverse**3 * (jnp.sum(cross, axis=-1, keepdims=True) / width)
    chunk = 4 * LANES
    for start in range(0, width, chunk):
        at = slice(start, start + chunk)
        term = inverse * term_ref[:, at] - layers_ref[:, :, at].reshape(rows, chunk) * back
        sums = [term[(sections - 1) * step :]]
        for s in reversed(range(sections - 1)):
            sums.insert(0, sums[0] + term[s * step : (s + 1) * step])
        out_ref[:, at] = jnp.concatenate(sums, axis=0).astype(BF16)


def finish(pages, weights, hidden, norm_gain, upper_grad):
    prompt_count, width = upper_grad.shape
    sections, quarter, _ = hidden[0].shape
    members = pages.shape[0]
    scaled = pl.pallas_call(
        project_kernel,
        out_shape=jax.ShapeDtypeStruct((members * prompt_count, width // members), BF16),
        scratch_shapes=[
            pltpu.VMEM((width // (2 * LANES), 2 * LANES), F32),
            pltpu.VMEM((2, lax.axis_size("y")) + weights[0].shape, BF16),
        ],
        compiler_params=SMALL,
        cost_estimate=pl.CostEstimate(flops=3 * 10**8, bytes_accessed=2 * 10**6, transcendentals=0),
        name="projection",
    )(pages.reshape(-1, WIDE), *weights, norm_gain)
    scaled = scaled.reshape(members * sections, quarter, -1)
    scaled = lax.all_to_all(scaled, ("z", "section"), split_axis=0, concat_axis=0, tiled=True)
    sums = pl.pallas_call(
        term_kernel,
        out_shape=jax.ShapeDtypeStruct((prompt_count, width), BF16),
        scratch_shapes=[pltpu.VMEM((prompt_count, width), F32), pltpu.VMEM((sections, quarter, width), F32)],
        compiler_params=SMALL,
        cost_estimate=pl.CostEstimate(flops=10**8, bytes_accessed=10**6, transcendentals=0),
        name="norm_terms",
    )(scaled.reshape(members, prompt_count, -1), *hidden)
    sums = lax.all_to_all(sums.reshape(sections, quarter, width), "section", split_axis=0, concat_axis=0, tiled=True)
    return (upper_grad.astype(F32) + sums.reshape(prompt_count, width).astype(F32)).astype(BF16)


def swap(piece):
    return lax.ppermute(piece, "core", [(0, 1), (1, 0)])


def turn(piece, axis, k):
    size = lax.axis_size(axis)
    return lax.ppermute(piece, axis, [(i, (i + k) % size) for i in range(size)])


def part_ways(piece, j):
    rows = lax.axis_size("y")
    pairs = [(2 * y + c, (y + (j if c == 0 else rows - j)) % rows * 2 + c) for y in range(rows) for c in range(2)]
    return lax.ppermute(piece, ("y", "core"), pairs)


def hand_over(hidden, k):
    size, here = hidden.shape[0], lax.axis_index("section")
    return turn(lax.dynamic_index_in_dim(hidden, lax.rem(here + k, size), keepdims=False), "section", k)


def collect(pieces, block):
    count = sum(piece.shape[0] for piece in pieces) // block
    return pl.pallas_call(
        collect_kernel,
        out_shape=jax.ShapeDtypeStruct((count, block, WIDE), BF16),
        compiler_params=SMALL,
        cost_estimate=pl.CostEstimate(flops=0, bytes_accessed=10**6, transcendentals=0),
        name="weight_rows",
    )(*pieces)


def body(queries, out_grad, resp_kv, prompt_kv, prompt_hidden, norm_gain, kv_weight, upper_grad, group_list, lengths, owner_map):
    prompt_count, devices = owner_map.shape
    sections = lax.axis_size("section")
    width = prompt_hidden.shape[-1]
    score_grad, own_out, outgoing = attention(
        queries[0], out_grad[0], resp_kv[0], prompt_kv[0], group_list, lengths, owner_map
    )
    hidden = prompt_hidden[0].reshape(sections, prompt_count // sections, width)
    outgoing, weight, hidden = lax.optimization_barrier((outgoing, kv_weight[0], hidden))
    outgoing = outgoing.reshape(devices, -1, WIDE // 2)
    incoming = lax.all_to_all(outgoing, RESP_AXES, split_axis=0, concat_axis=0, tiled=True)
    layers = [hidden, hand_over(hidden, 1)]
    sibling = swap(weight)
    both, hidden = lax.optimization_barrier((jnp.concatenate([weight, sibling], axis=0), hidden))
    near = [part_ways(both, 1), part_ways(both, 2)]
    layers += [hand_over(hidden, k) for k in range(2, sections)]
    query_out = query_gradient(score_grad, resp_kv[0], prompt_kv[0])
    incoming, both, near, layers, weight, query_out = lax.optimization_barrier(
        (incoming, both, near, layers, weight, query_out)
    )
    pages = pl.pallas_call(
        page_kernel,
        out_shape=jax.ShapeDtypeStruct((lax.axis_size("z"), prompt_count, WIDE), BF16),
        compiler_params=SMALL,
        cost_estimate=pl.CostEstimate(flops=10**8, bytes_accessed=10**6, transcendentals=0),
        name="page_sum",
    )(jnp.repeat(group_list, 2)[None, :], incoming.reshape(-1, WIDE // 2))
    pages = lax.all_to_all(pages, "z", split_axis=0, concat_axis=0, tiled=True)
    near += [part_ways(both, 3), turn(weight, "y", lax.axis_size("y") // 2)]
    near = collect(near, weight.shape[0])
    far = swap(near)
    prompt_out = finish(pages, [weight, sibling, near, far], layers, norm_gain, upper_grad)
    return (query_out[None], own_out[None], prompt_out[None])


def solution(mesh):
    wide = jax.sharding.Mesh(mesh.devices.reshape(8, 8, 2, mesh.shape["section"]), RESP_AXES + ("section",))
    in_specs = (
        P("section", RESP_AXES, None),
        P("section", RESP_AXES, None),
        P("section", RESP_AXES, None),
        P("section", RESP_AXES, None, None),
        P("section", RESP_AXES, None),
        P("section", None),
        P("section", RESP_AXES, None),
        P(RESP_AXES, None),
        P(),
        P(RESP_AXES),
        P(),
    )
    out_specs = (P("section", RESP_AXES, None),) * 3
    return jax.shard_map(body, mesh=wide, in_specs=in_specs, out_specs=out_specs, check_vma=False)
```

```python
import functools

import jax
import jax.numpy as jnp
from jax import lax
from jax.experimental import pallas as pl
from jax.experimental.pallas import tpu as pltpu
from jax.sharding import PartitionSpec as P

QH = 32
KVH = 4
HD = 128
PER = QH // KVH
RESP_DEV = 4
WIDE = 2 * KVH * HD
LOG2E = 1.4426950408889634
SMALL = pltpu.CompilerParams(vmem_limit_bytes=16 * 1024 * 1024)
F32 = jnp.float32
BF16 = jnp.bfloat16


def dot(a, b, dims):
    return lax.dot_general(a, b, (dims, ((), ())), preferred_element_type=F32)


RESP_AXES = ("z", "y", "core")
LANES = 128


def resp_index():
    index = 0
    for axis in RESP_AXES:
        index = index * lax.axis_size(axis) + lax.axis_index(axis)
    return index


def attention_kernel(groups, lengths, q_ref, do_ref, own_ref, cache_ref, owner_ref, grad_ref, down_ref, send_ref, mixed_ref):
    b = pl.program_id(0)
    count = RESP_DEV
    length = lengths[b]
    rows = q_ref.shape[0]
    plen = cache_ref.shape[0]
    scaling = HD ** (-0.5)
    lanes = PER * rows
    key_pos = lax.broadcasted_iota(jnp.int32, (rows, lanes), 0)
    query_pos = lax.broadcasted_iota(jnp.int32, (rows, lanes), 1) % rows
    allowed = (key_pos <= query_pos) & (key_pos < length)
    live = (lax.broadcasted_iota(jnp.int32, (rows, HD), 0) < length).astype(BF16)
    group = groups[resp_index() * count + b]
    owners = owner_ref[pl.ds(group, 1), :]
    devices = owner_ref.shape[1]
    place = (lax.broadcasted_iota(jnp.int32, (devices, devices), 0) == owners).astype(BF16)
    own_kv = own_ref[...]
    cached = cache_ref[...]
    heads = [slice(h * HD, (h + 1) * HD) for h in range(QH)]
    key_cols = heads[:KVH]
    value_cols = heads[KVH : 2 * KVH]
    each = range(KVH)
    q = [jnp.concatenate([q_ref[:, h] for h in heads[k * PER : (k + 1) * PER]], axis=0) for k in each]
    keys = [jnp.concatenate([cached[:, at], own_kv[:, at]], axis=0) for at in key_cols]
    scores = [dot(keys[k], q[k], ((1,), (1,))) for k in each]
    do = [jnp.concatenate([do_ref[:, h] * live for h in heads[k * PER : (k + 1) * PER]], axis=0) for k in each]
    values = [jnp.concatenate([cached[:, at], own_kv[:, at]], axis=0) for at in value_cols]
    prob_grad = [dot(values[k], do[k], ((1,), (1,))) for k in each]
    low, score_grad = [], []
    for k in each:
        masked = jnp.concatenate([scores[k][:plen], jnp.where(allowed, scores[k][plen:], -1e30)], axis=0)
        expo = jnp.exp2((masked - jnp.max(masked, axis=0, keepdims=True)) * (scaling * LOG2E))
        probs = expo * (1.0 / jnp.sum(expo, axis=0, keepdims=True))
        low.append(probs.astype(BF16))
        delta = jnp.sum(low[k].astype(F32) * prob_grad[k], axis=0, keepdims=True)
        score_grad.append((probs * ((prob_grad[k] - delta) * scaling)).astype(BF16))
    grads = []
    for k in each:
        grads.append((k, 1, value_cols[k], dot(low[k], do[k], ((1,), (0,)))))
        grads.append((k, 0, key_cols[k], dot(score_grad[k], q[k], ((1,), (0,)))))
    for k in each:
        grad_ref[k] = score_grad[k]
    for k, half, at, grad in grads:
        down_ref[:, at] = grad[plen:].astype(BF16)
        part = dot(place, grad[:plen].astype(BF16), ((1,), (0,)))
        mixed_ref[2 * b + half, :, k * HD : (k + 1) * HD] = part.astype(BF16)

    @pl.when(b == count - 1)
    def _():
        slots, step = 2 * count, 16
        size = slots * step
        row = lax.broadcasted_iota(jnp.int32, (size, size), 0)
        order = (lax.broadcasted_iota(jnp.int32, (size, size), 1) == row % slots * step + row // slots).astype(BF16)
        for start in range(0, devices, step):
            block = mixed_ref[:, start : start + step, :].reshape(size, mixed_ref.shape[2])
            send_ref[start * slots : start * slots + size, :] = dot(order, block, ((1,), (0,))).astype(BF16)


def attention(queries, out_grad, resp_kv, prompt_kv, group_list, lengths, owner_map):
    count, plen, _ = prompt_kv.shape
    total = queries.shape[0]
    rows = total // count
    width = queries.shape[1]
    keys, lanes = plen + rows, PER * rows
    by_resp = lambda w: pl.BlockSpec((rows, w), lambda b, *_: (b, 0))
    return pl.pallas_call(
        attention_kernel,
        grid_spec=pltpu.PrefetchScalarGridSpec(
            num_scalar_prefetch=2,
            grid=(count,),
            in_specs=[
                by_resp(width),
                by_resp(width),
                by_resp(WIDE),
                pl.BlockSpec((None, plen, WIDE), lambda b, *_: (b, 0, 0)),
                pl.BlockSpec(owner_map.shape, lambda b, *_: (0, 0)),
            ],
            out_specs=[
                pl.BlockSpec((KVH, keys, lanes), lambda b, *_: (b, 0, 0)),
                by_resp(WIDE),
                pl.BlockSpec((2 * count * plen, WIDE // 2), lambda b, *_: (0, 0)),
            ],
            scratch_shapes=[pltpu.VMEM((2 * count, plen, WIDE // 2), BF16)],
        ),
        out_shape=[
            jax.ShapeDtypeStruct((count * KVH, keys, lanes), BF16),
            jax.ShapeDtypeStruct((total, WIDE), BF16),
            jax.ShapeDtypeStruct((2 * count * plen, WIDE // 2), BF16),
        ],
        cost_estimate=pl.CostEstimate(flops=10**9, bytes_accessed=6 * 10**6, transcendentals=700000),
        name="attention_backward",
    )(group_list, lengths, queries, out_grad, resp_kv, prompt_kv, owner_map)


def query_kernel(grad_ref, own_ref, cache_ref, dq_ref):
    rows = dq_ref.shape[0]
    for k in range(KVH):
        at = slice(k * HD, (k + 1) * HD)
        keys = jnp.concatenate([cache_ref[:, at], own_ref[:, at]], axis=0)
        dq = dot(grad_ref[k], keys, ((0,), (0,)))
        for g in range(PER):
            h = k * PER + g
            dq_ref[:, h * HD : (h + 1) * HD] = dq[g * rows : (g + 1) * rows].astype(BF16)


def query_gradient(score_grad, resp_kv, prompt_kv):
    count, plen, _ = prompt_kv.shape
    total = resp_kv.shape[0]
    rows = total // count
    half = KVH * HD
    return pl.pallas_call(
        query_kernel,
        grid=(count,),
        in_specs=[
            pl.BlockSpec((KVH,) + score_grad.shape[1:], lambda b: (b, 0, 0)),
            pl.BlockSpec((rows, half), lambda b: (b, 0)),
            pl.BlockSpec((None, plen, half), lambda b: (b, 0, 0)),
        ],
        out_specs=pl.BlockSpec((rows, QH * HD), lambda b: (b, 0)),
        out_shape=jax.ShapeDtypeStruct((total, QH * HD), BF16),
        cost_estimate=pl.CostEstimate(flops=2 * 10**8, bytes_accessed=4 * 10**6, transcendentals=0),
        name="query_gradient",
    )(score_grad, resp_kv, prompt_kv)


def page_kernel(groups_ref, arrived_ref, page_ref):
    copies, prompts, _ = page_ref.shape
    rows, half = arrived_ref.shape
    ids = lax.broadcasted_iota(jnp.int32, (2 * prompts, rows), 0)
    odd = lax.broadcasted_iota(jnp.int32, (2 * prompts, rows), 1) % 2
    select = (ids == groups_ref[...] + prompts * odd).astype(BF16)
    page = dot(select, arrived_ref[...], ((1,), (0,))).astype(BF16)
    for copy in range(copies):
        page_ref[copy, :, :half] = page[:prompts]
        page_ref[copy, :, half:] = page[prompts:]


def natural_order(transposed):
    span = 2 * LANES
    held = lax.broadcasted_iota(jnp.int32, (span, span), 1 if transposed else 0)
    model = lax.broadcasted_iota(jnp.int32, (span, span), 0 if transposed else 1)
    rows = 32
    core, rest = held // LANES, held % LANES
    return (model == rest // rows * (2 * rows) + core * rows + rest % rows).astype(BF16)


def collect_kernel(*refs):
    out_ref, pieces = refs[-1], refs[:-1]
    block, at = out_ref.shape[1], 0
    for ref in pieces:
        for start in range(0, ref.shape[0], block):
            out_ref[at] = ref[start : start + block]
            at += 1


def project_kernel(pages_ref, own_ref, sibling_ref, near_ref, far_ref, gain_ref, out_ref, gain_rows, weight_ref):
    span = 2 * LANES
    gain = gain_ref[...].astype(F32)
    gain = jnp.concatenate([gain[:, start : start + span] for start in range(0, gain.shape[1], span)], axis=0)
    gain_rows[...] = dot(gain.astype(BF16), natural_order(True), ((1,), (0,)))
    cores, rows, block, _ = weight_ref.shape
    core, row = lax.axis_index("core"), lax.axis_index("y")
    other = 1 - core
    weight_ref[core, row] = own_ref[...]
    weight_ref[other, row] = sibling_ref[...]
    for j in range(1, rows // 2):
        below = lax.rem(row + rows - j, rows)
        above = lax.rem(row + j, rows)
        near = jnp.where(core == 0, below, above)
        far = jnp.where(core == 0, above, below)
        weight_ref[core, near] = near_ref[2 * j - 2]
        weight_ref[other, near] = near_ref[2 * j - 1]
        weight_ref[other, far] = far_ref[2 * j - 2]
        weight_ref[core, far] = far_ref[2 * j - 1]
    middle = lax.rem(row + rows // 2, rows)
    weight_ref[core, middle] = near_ref[rows - 2]
    weight_ref[other, middle] = far_ref[rows - 2]
    cols = rows * block
    pairs = cols // LANES
    scales = [gain_rows[pl.ds(lax.axis_index("z") * pairs + pair, 1), :] for pair in range(pairs)]
    for c in range(cores):
        normed = dot(pages_ref[...], weight_ref[c].reshape(cols, WIDE), ((1,), (1,)))
        for pair in range(pairs):
            at = slice(pair * LANES, (pair + 1) * LANES)
            start = c * cols + pair * LANES
            out_ref[:, start : start + LANES] = (normed[:, at] * scales[pair][:, c * LANES : (c + 1) * LANES]).astype(BF16)


def term_kernel(scaled_ref, hidden_ref, *refs):
    got, (out_ref, term_ref, layers_ref) = refs[:-3], refs[-3:]
    blocks, rows, cols = scaled_ref.shape
    sections, step, width = layers_ref.shape
    here = lax.axis_index("section")
    layers_ref[here] = hidden_ref[here].astype(F32)
    for k, ref in enumerate(got, 1):
        layers_ref[lax.rem(here + sections - k, sections)] = ref[...].astype(F32)
    span = 2 * LANES
    pairs = cols // span
    mixed = []
    for block in range(blocks):
        for pair in range(pairs):
            low, high = pair * LANES, (pairs + pair) * LANES
            mixed.append(
                jnp.concatenate([scaled_ref[block, :, low : low + LANES], scaled_ref[block, :, high : high + LANES]], axis=1)
            )
    scaled = dot(jnp.concatenate(mixed, axis=0), natural_order(False), ((1,), (0,)))
    squares = jnp.zeros((rows, span), F32)
    cross = jnp.zeros((rows, span), F32)
    for n in range(len(mixed)):
        at = slice(n * span, (n + 1) * span)
        part = scaled[n * rows : (n + 1) * rows]
        term_ref[:, at] = part
        hidden = layers_ref[:, :, at].reshape(rows, span)
        squares += hidden * hidden
        cross += hidden * part
    inverse = lax.rsqrt(jnp.sum(squares, axis=-1, keepdims=True) / width + 1e-06)
    back = inverse**3 * (jnp.sum(cross, axis=-1, keepdims=True) / width)
    chunk = 4 * LANES
    for start in range(0, width, chunk):
        at = slice(start, start + chunk)
        term = inverse * term_ref[:, at] - layers_ref[:, :, at].reshape(rows, chunk) * back
        sums = [term[(sections - 1) * step :]]
        for s in reversed(range(sections - 1)):
            sums.insert(0, sums[0] + term[s * step : (s + 1) * step])
        out_ref[:, at] = jnp.concatenate(sums, axis=0).astype(BF16)


def finish(pages, weights, hidden, norm_gain, upper_grad):
    prompt_count, width = upper_grad.shape
    sections, quarter, _ = hidden[0].shape
    members = pages.shape[0]
    scaled = pl.pallas_call(
        project_kernel,
        out_shape=jax.ShapeDtypeStruct((members * prompt_count, width // members), BF16),
        scratch_shapes=[
            pltpu.VMEM((width // (2 * LANES), 2 * LANES), F32),
            pltpu.VMEM((2, lax.axis_size("y")) + weights[0].shape, BF16),
        ],
        compiler_params=SMALL,
        cost_estimate=pl.CostEstimate(flops=3 * 10**8, bytes_accessed=2 * 10**6, transcendentals=0),
        name="projection",
    )(pages.reshape(-1, WIDE), *weights, norm_gain)
    scaled = scaled.reshape(members * sections, quarter, -1)
    scaled = lax.all_to_all(scaled, ("z", "section"), split_axis=0, concat_axis=0, tiled=True)
    sums = pl.pallas_call(
        term_kernel,
        out_shape=jax.ShapeDtypeStruct((prompt_count, width), BF16),
        scratch_shapes=[pltpu.VMEM((prompt_count, width), F32), pltpu.VMEM((sections, quarter, width), F32)],
        compiler_params=SMALL,
        cost_estimate=pl.CostEstimate(flops=10**8, bytes_accessed=10**6, transcendentals=0),
        name="norm_terms",
    )(scaled.reshape(members, prompt_count, -1), *hidden)
    sums = lax.all_to_all(sums.reshape(sections, quarter, width), "section", split_axis=0, concat_axis=0, tiled=True)
    return (upper_grad.astype(F32) + sums.reshape(prompt_count, width).astype(F32)).astype(BF16)


def swap(piece):
    return lax.ppermute(piece, "core", [(0, 1), (1, 0)])


def turn(piece, axis, k):
    size = lax.axis_size(axis)
    return lax.ppermute(piece, axis, [(i, (i + k) % size) for i in range(size)])


def part_ways(piece, j):
    rows = lax.axis_size("y")
    pairs = [(2 * y + c, (y + (j if c == 0 else rows - j)) % rows * 2 + c) for y in range(rows) for c in range(2)]
    return lax.ppermute(piece, ("y", "core"), pairs)


def hand_over(hidden, k):
    size, here = hidden.shape[0], lax.axis_index("section")
    return turn(lax.dynamic_index_in_dim(hidden, lax.rem(here + k, size), keepdims=False), "section", k)


def collect(pieces, block):
    count = sum(piece.shape[0] for piece in pieces) // block
    return pl.pallas_call(
        collect_kernel,
        out_shape=jax.ShapeDtypeStruct((count, block, WIDE), BF16),
        compiler_params=SMALL,
        cost_estimate=pl.CostEstimate(flops=0, bytes_accessed=10**6, transcendentals=0),
        name="weight_rows",
    )(*pieces)


def body(queries, out_grad, resp_kv, prompt_kv, prompt_hidden, norm_gain, kv_weight, upper_grad, group_list, lengths, owner_map):
    prompt_count, devices = owner_map.shape
    sections = lax.axis_size("section")
    width = prompt_hidden.shape[-1]
    score_grad, own_out, outgoing = attention(
        queries[0], out_grad[0], resp_kv[0], prompt_kv[0], group_list, lengths, owner_map
    )
    hidden = prompt_hidden[0].reshape(sections, prompt_count // sections, width)
    outgoing, weight, hidden = lax.optimization_barrier((outgoing, kv_weight[0], hidden))
    outgoing = outgoing.reshape(devices, -1, WIDE // 2)
    incoming = lax.all_to_all(outgoing, RESP_AXES, split_axis=0, concat_axis=0, tiled=True)
    layers = [hidden, hand_over(hidden, 1)]
    sibling = swap(weight)
    both, hidden = lax.optimization_barrier((jnp.concatenate([weight, sibling], axis=0), hidden))
    near = [part_ways(both, 1), part_ways(both, 2)]
    layers += [hand_over(hidden, k) for k in range(2, sections)]
    query_out = query_gradient(score_grad, resp_kv[0], prompt_kv[0])
    incoming, both, near, layers, weight, query_out = lax.optimization_barrier(
        (incoming, both, near, layers, weight, query_out)
    )
    pages = pl.pallas_call(
        page_kernel,
        out_shape=jax.ShapeDtypeStruct((lax.axis_size("z"), prompt_count, WIDE), BF16),
        compiler_params=SMALL,
        cost_estimate=pl.CostEstimate(flops=10**8, bytes_accessed=10**6, transcendentals=0),
        name="page_sum",
    )(jnp.repeat(group_list, 2)[None, :], incoming.reshape(-1, WIDE // 2))
    pages = lax.all_to_all(pages, "z", split_axis=0, concat_axis=0, tiled=True)
    near += [part_ways(both, 3), turn(weight, "y", lax.axis_size("y") // 2)]
    near = collect(near, weight.shape[0])
    far = swap(near)
    prompt_out = finish(pages, [weight, sibling, near, far], layers, norm_gain, upper_grad)
    return (query_out[None], own_out[None], prompt_out[None])


def solution(mesh):
    wide = jax.sharding.Mesh(mesh.devices.reshape(8, 8, 2, mesh.shape["section"]), RESP_AXES + ("section",))
    in_specs = (
        P("section", RESP_AXES, None),
        P("section", RESP_AXES, None),
        P("section", RESP_AXES, None),
        P("section", RESP_AXES, None, None),
        P("section", RESP_AXES, None),
        P("section", None),
        P("section", RESP_AXES, None),
        P(RESP_AXES, None),
        P(),
        P(RESP_AXES),
        P(),
    )
    out_specs = (P("section", RESP_AXES, None),) * 3
    return jax.shard_map(body, mesh=wide, in_specs=in_specs, out_specs=out_specs, check_vma=False)
```

```python
import functools

import jax
import jax.numpy as jnp
from jax import lax
from jax.experimental import pallas as pl
from jax.experimental.pallas import tpu as pltpu
from jax.sharding import PartitionSpec as P

QH = 32
KVH = 4
HD = 128
PER = QH // KVH
RESP_DEV = 4
WIDE = 2 * KVH * HD
LOG2E = 1.4426950408889634
SMALL = pltpu.CompilerParams(vmem_limit_bytes=16 * 1024 * 1024)
F32 = jnp.float32
BF16 = jnp.bfloat16


def dot(a, b, dims):
    return lax.dot_general(a, b, (dims, ((), ())), preferred_element_type=F32)


RESP_AXES = ("z", "y", "core")
LANES = 128


def resp_index():
    index = 0
    for axis in RESP_AXES:
        index = index * lax.axis_size(axis) + lax.axis_index(axis)
    return index


def attention_kernel(groups, lengths, q_ref, do_ref, own_ref, cache_ref, owner_ref, grad_ref, down_ref, send_ref, mixed_ref):
    b = pl.program_id(0)
    count = RESP_DEV
    length = lengths[b]
    rows = q_ref.shape[0]
    plen = cache_ref.shape[0]
    scaling = HD ** (-0.5)
    lanes = PER * rows
    key_pos = lax.broadcasted_iota(jnp.int32, (rows, lanes), 0)
    query_pos = lax.broadcasted_iota(jnp.int32, (rows, lanes), 1) % rows
    allowed = (key_pos <= query_pos) & (key_pos < length)
    live = (lax.broadcasted_iota(jnp.int32, (rows, HD), 0) < length).astype(BF16)
    group = groups[resp_index() * count + b]
    owners = owner_ref[pl.ds(group, 1), :]
    devices = owner_ref.shape[1]
    place = (lax.broadcasted_iota(jnp.int32, (devices, devices), 0) == owners).astype(BF16)
    own_kv = own_ref[...]
    cached = cache_ref[...]
    heads = [slice(h * HD, (h + 1) * HD) for h in range(QH)]
    key_cols = heads[:KVH]
    value_cols = heads[KVH : 2 * KVH]
    each = range(KVH)
    q = [jnp.concatenate([q_ref[:, h] for h in heads[k * PER : (k + 1) * PER]], axis=0) for k in each]
    keys = [jnp.concatenate([cached[:, at], own_kv[:, at]], axis=0) for at in key_cols]
    scores = [dot(keys[k], q[k], ((1,), (1,))) for k in each]
    do = [jnp.concatenate([do_ref[:, h] * live for h in heads[k * PER : (k + 1) * PER]], axis=0) for k in each]
    values = [jnp.concatenate([cached[:, at], own_kv[:, at]], axis=0) for at in value_cols]
    prob_grad = [dot(values[k], do[k], ((1,), (1,))) for k in each]
    low, score_grad = [], []
    for k in each:
        masked = jnp.concatenate([scores[k][:plen], jnp.where(allowed, scores[k][plen:], -1e30)], axis=0)
        expo = jnp.exp2((masked - jnp.max(masked, axis=0, keepdims=True)) * (scaling * LOG2E))
        probs = expo * (1.0 / jnp.sum(expo, axis=0, keepdims=True))
        low.append(probs.astype(BF16))
        delta = jnp.sum(low[k].astype(F32) * prob_grad[k], axis=0, keepdims=True)
        score_grad.append((probs * ((prob_grad[k] - delta) * scaling)).astype(BF16))
    grads = []
    for k in each:
        grads.append((k, 1, value_cols[k], dot(low[k], do[k], ((1,), (0,)))))
        grads.append((k, 0, key_cols[k], dot(score_grad[k], q[k], ((1,), (0,)))))
    for k in each:
        grad_ref[k] = score_grad[k]
    for k, half, at, grad in grads:
        down_ref[:, at] = grad[plen:].astype(BF16)
        part = dot(place, grad[:plen].astype(BF16), ((1,), (0,)))
        mixed_ref[k, pl.ds(2 * b + half, devices, stride=2 * count), :] = part

    @pl.when(b == count - 1)
    def _():
        for k in range(KVH):
            send_ref[:, k * HD : (k + 1) * HD] = mixed_ref[k].astype(BF16)


def attention(queries, out_grad, resp_kv, prompt_kv, group_list, lengths, owner_map):
    count, plen, _ = prompt_kv.shape
    total = queries.shape[0]
    rows = total // count
    width = queries.shape[1]
    keys, lanes = plen + rows, PER * rows
    by_resp = lambda w: pl.BlockSpec((rows, w), lambda b, *_: (b, 0))
    return pl.pallas_call(
        attention_kernel,
        grid_spec=pltpu.PrefetchScalarGridSpec(
            num_scalar_prefetch=2,
            grid=(count,),
            in_specs=[
                by_resp(width),
                by_resp(width),
                by_resp(WIDE),
                pl.BlockSpec((None, plen, WIDE), lambda b, *_: (b, 0, 0)),
                pl.BlockSpec(owner_map.shape, lambda b, *_: (0, 0)),
            ],
            out_specs=[
                pl.BlockSpec((KVH, keys, lanes), lambda b, *_: (b, 0, 0)),
                by_resp(WIDE),
                pl.BlockSpec((2 * count * plen, WIDE // 2), lambda b, *_: (0, 0)),
            ],
            scratch_shapes=[pltpu.VMEM((KVH, 2 * count * plen, HD), F32)],
        ),
        out_shape=[
            jax.ShapeDtypeStruct((count * KVH, keys, lanes), BF16),
            jax.ShapeDtypeStruct((total, WIDE), BF16),
            jax.ShapeDtypeStruct((2 * count * plen, WIDE // 2), BF16),
        ],
        cost_estimate=pl.CostEstimate(flops=10**9, bytes_accessed=6 * 10**6, transcendentals=700000),
        name="attention_backward",
    )(group_list, lengths, queries, out_grad, resp_kv, prompt_kv, owner_map)


def query_kernel(grad_ref, own_ref, cache_ref, dq_ref):
    rows = dq_ref.shape[0]
    for k in range(KVH):
        at = slice(k * HD, (k + 1) * HD)
        keys = jnp.concatenate([cache_ref[:, at], own_ref[:, at]], axis=0)
        dq = dot(grad_ref[k], keys, ((0,), (0,)))
        for g in range(PER):
            h = k * PER + g
            dq_ref[:, h * HD : (h + 1) * HD] = dq[g * rows : (g + 1) * rows].astype(BF16)


def query_gradient(score_grad, resp_kv, prompt_kv):
    count, plen, _ = prompt_kv.shape
    total = resp_kv.shape[0]
    rows = total // count
    half = KVH * HD
    return pl.pallas_call(
        query_kernel,
        grid=(count,),
        in_specs=[
            pl.BlockSpec((KVH,) + score_grad.shape[1:], lambda b: (b, 0, 0)),
            pl.BlockSpec((rows, half), lambda b: (b, 0)),
            pl.BlockSpec((None, plen, half), lambda b: (b, 0, 0)),
        ],
        out_specs=pl.BlockSpec((rows, QH * HD), lambda b: (b, 0)),
        out_shape=jax.ShapeDtypeStruct((total, QH * HD), BF16),
        cost_estimate=pl.CostEstimate(flops=2 * 10**8, bytes_accessed=4 * 10**6, transcendentals=0),
        name="query_gradient",
    )(score_grad, resp_kv, prompt_kv)


def page_kernel(groups_ref, arrived_ref, page_ref):
    copies, prompts, _ = page_ref.shape
    rows, half = arrived_ref.shape
    ids = lax.broadcasted_iota(jnp.int32, (2 * prompts, rows), 0)
    odd = lax.broadcasted_iota(jnp.int32, (2 * prompts, rows), 1) % 2
    select = (ids == groups_ref[...] + prompts * odd).astype(BF16)
    page = dot(select, arrived_ref[...], ((1,), (0,))).astype(BF16)
    for copy in range(copies):
        page_ref[copy, :, :half] = page[:prompts]
        page_ref[copy, :, half:] = page[prompts:]


def natural_order(transposed):
    span = 2 * LANES
    held = lax.broadcasted_iota(jnp.int32, (span, span), 1 if transposed else 0)
    model = lax.broadcasted_iota(jnp.int32, (span, span), 0 if transposed else 1)
    rows = 32
    core, rest = held // LANES, held % LANES
    return (model == rest // rows * (2 * rows) + core * rows + rest % rows).astype(BF16)


def collect_kernel(*refs):
    out_ref, pieces = refs[-1], refs[:-1]
    block, at = out_ref.shape[1], 0
    for ref in pieces:
        for start in range(0, ref.shape[0], block):
            out_ref[at] = ref[start : start + block]
            at += 1


def project_kernel(pages_ref, own_ref, sibling_ref, near_ref, far_ref, gain_ref, out_ref, gain_rows, weight_ref):
    span = 2 * LANES
    gain = gain_ref[...].astype(F32)
    gain = jnp.concatenate([gain[:, start : start + span] for start in range(0, gain.shape[1], span)], axis=0)
    gain_rows[...] = dot(gain.astype(BF16), natural_order(True), ((1,), (0,)))
    cores, rows, block, _ = weight_ref.shape
    core, row = lax.axis_index("core"), lax.axis_index("y")
    other = 1 - core
    weight_ref[core, row] = own_ref[...]
    weight_ref[other, row] = sibling_ref[...]
    for j in range(1, rows // 2):
        below = lax.rem(row + rows - j, rows)
        above = lax.rem(row + j, rows)
        near = jnp.where(core == 0, below, above)
        far = jnp.where(core == 0, above, below)
        weight_ref[core, near] = near_ref[2 * j - 2]
        weight_ref[other, near] = near_ref[2 * j - 1]
        weight_ref[other, far] = far_ref[2 * j - 2]
        weight_ref[core, far] = far_ref[2 * j - 1]
    middle = lax.rem(row + rows // 2, rows)
    weight_ref[core, middle] = near_ref[rows - 2]
    weight_ref[other, middle] = far_ref[rows - 2]
    cols = rows * block
    pairs = cols // LANES
    scales = [gain_rows[pl.ds(lax.axis_index("z") * pairs + pair, 1), :] for pair in range(pairs)]
    for c in range(cores):
        normed = dot(pages_ref[...], weight_ref[c].reshape(cols, WIDE), ((1,), (1,)))
        for pair in range(pairs):
            at = slice(pair * LANES, (pair + 1) * LANES)
            start = c * cols + pair * LANES
            out_ref[:, start : start + LANES] = (normed[:, at] * scales[pair][:, c * LANES : (c + 1) * LANES]).astype(BF16)


def term_kernel(scaled_ref, hidden_ref, *refs):
    got, (out_ref, term_ref, layers_ref) = refs[:-3], refs[-3:]
    blocks, rows, cols = scaled_ref.shape
    sections, step, width = layers_ref.shape
    here = lax.axis_index("section")
    layers_ref[here] = hidden_ref[here].astype(F32)
    for k, ref in enumerate(got, 1):
        layers_ref[lax.rem(here + sections - k, sections)] = ref[...].astype(F32)
    span = 2 * LANES
    pairs = cols // span
    mixed = []
    for block in range(blocks):
        for pair in range(pairs):
            low, high = pair * LANES, (pairs + pair) * LANES
            mixed.append(
                jnp.concatenate([scaled_ref[block, :, low : low + LANES], scaled_ref[block, :, high : high + LANES]], axis=1)
            )
    scaled = dot(jnp.concatenate(mixed, axis=0), natural_order(False), ((1,), (0,)))
    squares = jnp.zeros((rows, span), F32)
    cross = jnp.zeros((rows, span), F32)
    for n in range(len(mixed)):
        at = slice(n * span, (n + 1) * span)
        part = scaled[n * rows : (n + 1) * rows]
        term_ref[:, at] = part
        hidden = layers_ref[:, :, at].reshape(rows, span)
        squares += hidden * hidden
        cross += hidden * part
    inverse = lax.rsqrt(jnp.sum(squares, axis=-1, keepdims=True) / width + 1e-06)
    back = inverse**3 * (jnp.sum(cross, axis=-1, keepdims=True) / width)
    chunk = 4 * LANES
    for start in range(0, width, chunk):
        at = slice(start, start + chunk)
        term = inverse * term_ref[:, at] - layers_ref[:, :, at].reshape(rows, chunk) * back
        sums = [term[(sections - 1) * step :]]
        for s in reversed(range(sections - 1)):
            sums.insert(0, sums[0] + term[s * step : (s + 1) * step])
        out_ref[:, at] = jnp.concatenate(sums, axis=0).astype(BF16)


def finish(pages, weights, hidden, norm_gain, upper_grad):
    prompt_count, width = upper_grad.shape
    sections, quarter, _ = hidden[0].shape
    members = pages.shape[0]
    scaled = pl.pallas_call(
        project_kernel,
        out_shape=jax.ShapeDtypeStruct((members * prompt_count, width // members), BF16),
        scratch_shapes=[
            pltpu.VMEM((width // (2 * LANES), 2 * LANES), F32),
            pltpu.VMEM((2, lax.axis_size("y")) + weights[0].shape, BF16),
        ],
        compiler_params=SMALL,
        cost_estimate=pl.CostEstimate(flops=3 * 10**8, bytes_accessed=2 * 10**6, transcendentals=0),
        name="projection",
    )(pages.reshape(-1, WIDE), *weights, norm_gain)
    scaled = scaled.reshape(members * sections, quarter, -1)
    scaled = lax.all_to_all(scaled, ("z", "section"), split_axis=0, concat_axis=0, tiled=True)
    sums = pl.pallas_call(
        term_kernel,
        out_shape=jax.ShapeDtypeStruct((prompt_count, width), BF16),
        scratch_shapes=[pltpu.VMEM((prompt_count, width), F32), pltpu.VMEM((sections, quarter, width), F32)],
        compiler_params=SMALL,
        cost_estimate=pl.CostEstimate(flops=10**8, bytes_accessed=10**6, transcendentals=0),
        name="norm_terms",
    )(scaled.reshape(members, prompt_count, -1), *hidden)
    sums = lax.all_to_all(sums.reshape(sections, quarter, width), "section", split_axis=0, concat_axis=0, tiled=True)
    return (upper_grad.astype(F32) + sums.reshape(prompt_count, width).astype(F32)).astype(BF16)


def swap(piece):
    return lax.ppermute(piece, "core", [(0, 1), (1, 0)])


def turn(piece, axis, k):
    size = lax.axis_size(axis)
    return lax.ppermute(piece, axis, [(i, (i + k) % size) for i in range(size)])


def part_ways(piece, j):
    rows = lax.axis_size("y")
    pairs = [(2 * y + c, (y + (j if c == 0 else rows - j)) % rows * 2 + c) for y in range(rows) for c in range(2)]
    return lax.ppermute(piece, ("y", "core"), pairs)


def hand_over(hidden, k):
    size, here = hidden.shape[0], lax.axis_index("section")
    return turn(lax.dynamic_index_in_dim(hidden, lax.rem(here + k, size), keepdims=False), "section", k)


def collect(pieces, block):
    count = sum(piece.shape[0] for piece in pieces) // block
    return pl.pallas_call(
        collect_kernel,
        out_shape=jax.ShapeDtypeStruct((count, block, WIDE), BF16),
        compiler_params=SMALL,
        cost_estimate=pl.CostEstimate(flops=0, bytes_accessed=10**6, transcendentals=0),
        name="weight_rows",
    )(*pieces)


def body(queries, out_grad, resp_kv, prompt_kv, prompt_hidden, norm_gain, kv_weight, upper_grad, group_list, lengths, owner_map):
    prompt_count, devices = owner_map.shape
    sections = lax.axis_size("section")
    width = prompt_hidden.shape[-1]
    middle = turn(kv_weight[0], "y", lax.axis_size("y") // 2)
    score_grad, own_out, outgoing = attention(
        queries[0], out_grad[0], resp_kv[0], prompt_kv[0], group_list, lengths, owner_map
    )
    hidden = prompt_hidden[0].reshape(sections, prompt_count // sections, width)
    outgoing, weight, hidden = lax.optimization_barrier((outgoing, kv_weight[0], hidden))
    outgoing = outgoing.reshape(devices, -1, WIDE // 2)
    incoming = lax.all_to_all(outgoing, RESP_AXES, split_axis=0, concat_axis=0, tiled=True)
    sibling = swap(weight)
    both, hidden = lax.optimization_barrier((jnp.concatenate([weight, sibling], axis=0), hidden))
    near = [part_ways(both, 1), part_ways(both, 2)]
    layers = [hidden] + [hand_over(hidden, k) for k in range(1, sections)]
    query_out = query_gradient(score_grad, resp_kv[0], prompt_kv[0])
    incoming, both, near, layers, middle, query_out = lax.optimization_barrier(
        (incoming, both, near, layers, middle, query_out)
    )
    pages = pl.pallas_call(
        page_kernel,
        out_shape=jax.ShapeDtypeStruct((lax.axis_size("z"), prompt_count, WIDE), BF16),
        compiler_params=SMALL,
        cost_estimate=pl.CostEstimate(flops=10**8, bytes_accessed=10**6, transcendentals=0),
        name="page_sum",
    )(jnp.repeat(group_list, 2)[None, :], incoming.reshape(-1, WIDE // 2))
    pages = lax.all_to_all(pages, "z", split_axis=0, concat_axis=0, tiled=True)
    near = collect(near + [part_ways(both, 3), middle], weight.shape[0])
    far = swap(near)
    prompt_out = finish(pages, [weight, sibling, near, far], layers, norm_gain, upper_grad)
    return (query_out[None], own_out[None], prompt_out[None])


def solution(mesh):
    wide = jax.sharding.Mesh(mesh.devices.reshape(8, 8, 2, mesh.shape["section"]), RESP_AXES + ("section",))
    in_specs = (
        P("section", RESP_AXES, None),
        P("section", RESP_AXES, None),
        P("section", RESP_AXES, None),
        P("section", RESP_AXES, None, None),
        P("section", RESP_AXES, None),
        P("section", None),
        P("section", RESP_AXES, None),
        P(RESP_AXES, None),
        P(),
        P(RESP_AXES),
        P(),
    )
    out_specs = (P("section", RESP_AXES, None),) * 3
    return jax.shard_map(body, mesh=wide, in_specs=in_specs, out_specs=out_specs, check_vma=False)
```

```python
import functools

import jax
import jax.numpy as jnp
from jax import lax
from jax.experimental import pallas as pl
from jax.experimental.pallas import tpu as pltpu
from jax.sharding import PartitionSpec as P

QH = 32
KVH = 4
HD = 128
PER = QH // KVH
RESP_DEV = 4
WIDE = 2 * KVH * HD
LOG2E = 1.4426950408889634
SMALL = pltpu.CompilerParams(vmem_limit_bytes=16 * 1024 * 1024)
F32 = jnp.float32
BF16 = jnp.bfloat16


def dot(a, b, dims):
    return lax.dot_general(a, b, (dims, ((), ())), preferred_element_type=F32)


RESP_AXES = ("z", "y", "core")
LANES = 128


def resp_index():
    index = 0
    for axis in RESP_AXES:
        index = index * lax.axis_size(axis) + lax.axis_index(axis)
    return index


def attention_kernel(groups, lengths, q_ref, do_ref, own_ref, cache_ref, owner_ref, grad_ref, down_ref, send_ref, mixed_ref):
    b = pl.program_id(0)
    count = RESP_DEV
    length = lengths[b]
    rows = q_ref.shape[0]
    plen = cache_ref.shape[0]
    scaling = HD ** (-0.5)
    lanes = PER * rows
    key_pos = lax.broadcasted_iota(jnp.int32, (rows, lanes), 0)
    query_pos = lax.broadcasted_iota(jnp.int32, (rows, lanes), 1) % rows
    allowed = (key_pos <= query_pos) & (key_pos < length)
    live = (lax.broadcasted_iota(jnp.int32, (rows, HD), 0) < length).astype(BF16)
    group = groups[resp_index() * count + b]
    owners = owner_ref[pl.ds(group, 1), :]
    devices = owner_ref.shape[1]
    place = (lax.broadcasted_iota(jnp.int32, (devices, devices), 0) == owners).astype(BF16)
    own_kv = own_ref[...]
    cached = cache_ref[...]
    heads = [slice(h * HD, (h + 1) * HD) for h in range(QH)]
    key_cols = heads[:KVH]
    value_cols = heads[KVH : 2 * KVH]
    each = range(KVH)
    q = [jnp.concatenate([q_ref[:, h] for h in heads[k * PER : (k + 1) * PER]], axis=0) for k in each]
    keys = [jnp.concatenate([cached[:, at], own_kv[:, at]], axis=0) for at in key_cols]
    scores = [dot(keys[k], q[k], ((1,), (1,))) for k in each]
    do = [jnp.concatenate([do_ref[:, h] * live for h in heads[k * PER : (k + 1) * PER]], axis=0) for k in each]
    values = [jnp.concatenate([cached[:, at], own_kv[:, at]], axis=0) for at in value_cols]
    prob_grad = [dot(values[k], do[k], ((1,), (1,))) for k in each]
    low, score_grad = [], []
    for k in each:
        masked = jnp.concatenate([scores[k][:plen], jnp.where(allowed, scores[k][plen:], -1e30)], axis=0)
        expo = jnp.exp2((masked - jnp.max(masked, axis=0, keepdims=True)) * (scaling * LOG2E))
        probs = expo * (1.0 / jnp.sum(expo, axis=0, keepdims=True))
        low.append(probs.astype(BF16))
        delta = jnp.sum(low[k].astype(F32) * prob_grad[k], axis=0, keepdims=True)
        score_grad.append((probs * ((prob_grad[k] - delta) * scaling)).astype(BF16))
    grads = []
    for k in each:
        grads.append((k, 1, value_cols[k], dot(low[k], do[k], ((1,), (0,)))))
        grads.append((k, 0, key_cols[k], dot(score_grad[k], q[k], ((1,), (0,)))))
    for k in each:
        grad_ref[k] = score_grad[k]
    for k, half, at, grad in grads:
        down_ref[:, at] = grad[plen:].astype(BF16)
        part = dot(place, grad[:plen].astype(BF16), ((1,), (0,)))
        mixed_ref[k, pl.ds(2 * b + half, devices, stride=2 * count), :] = part

    @pl.when(b == count - 1)
    def _():
        for k in range(KVH):
            send_ref[:, k * HD : (k + 1) * HD] = mixed_ref[k].astype(BF16)


def attention(queries, out_grad, resp_kv, prompt_kv, group_list, lengths, owner_map):
    count, plen, _ = prompt_kv.shape
    total = queries.shape[0]
    rows = total // count
    width = queries.shape[1]
    keys, lanes = plen + rows, PER * rows
    by_resp = lambda w: pl.BlockSpec((rows, w), lambda b, *_: (b, 0))
    return pl.pallas_call(
        attention_kernel,
        grid_spec=pltpu.PrefetchScalarGridSpec(
            num_scalar_prefetch=2,
            grid=(count,),
            in_specs=[
                by_resp(width),
                by_resp(width),
                by_resp(WIDE),
                pl.BlockSpec((None, plen, WIDE), lambda b, *_: (b, 0, 0)),
                pl.BlockSpec(owner_map.shape, lambda b, *_: (0, 0)),
            ],
            out_specs=[
                pl.BlockSpec((KVH, keys, lanes), lambda b, *_: (b, 0, 0)),
                by_resp(WIDE),
                pl.BlockSpec((2 * count * plen, WIDE // 2), lambda b, *_: (0, 0)),
            ],
            scratch_shapes=[pltpu.VMEM((KVH, 2 * count * plen, HD), F32)],
        ),
        out_shape=[
            jax.ShapeDtypeStruct((count * KVH, keys, lanes), BF16),
            jax.ShapeDtypeStruct((total, WIDE), BF16),
            jax.ShapeDtypeStruct((2 * count * plen, WIDE // 2), BF16),
        ],
        cost_estimate=pl.CostEstimate(flops=10**9, bytes_accessed=6 * 10**6, transcendentals=700000),
        name="attention_backward",
    )(group_list, lengths, queries, out_grad, resp_kv, prompt_kv, owner_map)


def query_kernel(grad_ref, own_ref, cache_ref, dq_ref):
    rows = dq_ref.shape[0]
    for k in range(KVH):
        at = slice(k * HD, (k + 1) * HD)
        keys = jnp.concatenate([cache_ref[:, at], own_ref[:, at]], axis=0)
        dq = dot(grad_ref[k], keys, ((0,), (0,)))
        for g in range(PER):
            h = k * PER + g
            dq_ref[:, h * HD : (h + 1) * HD] = dq[g * rows : (g + 1) * rows].astype(BF16)


def query_gradient(score_grad, resp_kv, prompt_kv):
    count, plen, _ = prompt_kv.shape
    total = resp_kv.shape[0]
    rows = total // count
    half = KVH * HD
    return pl.pallas_call(
        query_kernel,
        grid=(count,),
        in_specs=[
            pl.BlockSpec((KVH,) + score_grad.shape[1:], lambda b: (b, 0, 0)),
            pl.BlockSpec((rows, half), lambda b: (b, 0)),
            pl.BlockSpec((None, plen, half), lambda b: (b, 0, 0)),
        ],
        out_specs=pl.BlockSpec((rows, QH * HD), lambda b: (b, 0)),
        out_shape=jax.ShapeDtypeStruct((total, QH * HD), BF16),
        cost_estimate=pl.CostEstimate(flops=2 * 10**8, bytes_accessed=4 * 10**6, transcendentals=0),
        name="query_gradient",
    )(score_grad, resp_kv, prompt_kv)


def page_kernel(groups_ref, arrived_ref, page_ref):
    copies, prompts, _ = page_ref.shape
    rows, half = arrived_ref.shape
    ids = lax.broadcasted_iota(jnp.int32, (2 * prompts, rows), 0)
    odd = lax.broadcasted_iota(jnp.int32, (2 * prompts, rows), 1) % 2
    select = (ids == groups_ref[...] + prompts * odd).astype(BF16)
    page = dot(select, arrived_ref[...], ((1,), (0,))).astype(BF16)
    for copy in range(copies):
        page_ref[copy, :, :half] = page[:prompts]
        page_ref[copy, :, half:] = page[prompts:]


def natural_order(transposed):
    span = 2 * LANES
    held = lax.broadcasted_iota(jnp.int32, (span, span), 1 if transposed else 0)
    model = lax.broadcasted_iota(jnp.int32, (span, span), 0 if transposed else 1)
    rows = 32
    core, rest = held // LANES, held % LANES
    return (model == rest // rows * (2 * rows) + core * rows + rest % rows).astype(BF16)


def collect_kernel(*refs):
    out_ref, pieces = refs[-1], refs[:-1]
    block, at = out_ref.shape[1], 0
    for ref in pieces:
        for start in range(0, ref.shape[0], block):
            out_ref[at] = ref[start : start + block]
            at += 1


def project_kernel(pages_ref, own_ref, sibling_ref, near_ref, far_ref, gain_ref, out_ref, gain_rows, weight_ref):
    span = 2 * LANES
    gain = gain_ref[...].astype(F32)
    gain = jnp.concatenate([gain[:, start : start + span] for start in range(0, gain.shape[1], span)], axis=0)
    gain_rows[...] = dot(gain.astype(BF16), natural_order(True), ((1,), (0,)))
    cores, rows, block, _ = weight_ref.shape
    core, row = lax.axis_index("core"), lax.axis_index("y")
    other = 1 - core
    weight_ref[core, row] = own_ref[...]
    weight_ref[other, row] = sibling_ref[...]
    for j in range(1, rows // 2):
        below = lax.rem(row + rows - j, rows)
        above = lax.rem(row + j, rows)
        near = jnp.where(core == 0, below, above)
        far = jnp.where(core == 0, above, below)
        weight_ref[core, near] = near_ref[2 * j - 2]
        weight_ref[other, near] = near_ref[2 * j - 1]
        weight_ref[other, far] = far_ref[2 * j - 2]
        weight_ref[core, far] = far_ref[2 * j - 1]
    middle = lax.rem(row + rows // 2, rows)
    weight_ref[core, middle] = near_ref[rows - 2]
    weight_ref[other, middle] = far_ref[rows - 2]
    cols = rows * block
    pairs = cols // LANES
    scales = [gain_rows[pl.ds(lax.axis_index("z") * pairs + pair, 1), :] for pair in range(pairs)]
    for c in range(cores):
        normed = dot(pages_ref[...], weight_ref[c].reshape(cols, WIDE), ((1,), (1,)))
        for pair in range(pairs):
            at = slice(pair * LANES, (pair + 1) * LANES)
            start = c * cols + pair * LANES
            out_ref[:, start : start + LANES] = (normed[:, at] * scales[pair][:, c * LANES : (c + 1) * LANES]).astype(BF16)


def term_kernel(scaled_ref, hidden_ref, *refs):
    got, (out_ref, term_ref, layers_ref) = refs[:-3], refs[-3:]
    blocks, rows, cols = scaled_ref.shape
    sections, step, width = layers_ref.shape
    here = lax.axis_index("section")
    layers_ref[here] = hidden_ref[here].astype(F32)
    for k, ref in enumerate(got, 1):
        layers_ref[lax.rem(here + sections - k, sections)] = ref[...].astype(F32)
    span = 2 * LANES
    pairs = cols // span
    mixed = []
    for block in range(blocks):
        for pair in range(pairs):
            low, high = pair * LANES, (pairs + pair) * LANES
            mixed.append(
                jnp.concatenate([scaled_ref[block, :, low : low + LANES], scaled_ref[block, :, high : high + LANES]], axis=1)
            )
    scaled = dot(jnp.concatenate(mixed, axis=0), natural_order(False), ((1,), (0,)))
    squares = jnp.zeros((rows, span), F32)
    cross = jnp.zeros((rows, span), F32)
    for n in range(len(mixed)):
        at = slice(n * span, (n + 1) * span)
        part = scaled[n * rows : (n + 1) * rows]
        term_ref[:, at] = part
        hidden = layers_ref[:, :, at].reshape(rows, span)
        squares += hidden * hidden
        cross += hidden * part
    inverse = lax.rsqrt(jnp.sum(squares, axis=-1, keepdims=True) / width + 1e-06)
    back = inverse**3 * (jnp.sum(cross, axis=-1, keepdims=True) / width)
    chunk = 4 * LANES
    for start in range(0, width, chunk):
        at = slice(start, start + chunk)
        term = inverse * term_ref[:, at] - layers_ref[:, :, at].reshape(rows, chunk) * back
        sums = [term[(sections - 1) * step :]]
        for s in reversed(range(sections - 1)):
            sums.insert(0, sums[0] + term[s * step : (s + 1) * step])
        out_ref[:, at] = jnp.concatenate(sums, axis=0).astype(BF16)


def finish(pages, weights, hidden, norm_gain, upper_grad):
    prompt_count, width = upper_grad.shape
    sections, quarter, _ = hidden[0].shape
    members = pages.shape[0]
    scaled = pl.pallas_call(
        project_kernel,
        out_shape=jax.ShapeDtypeStruct((members * prompt_count, width // members), BF16),
        scratch_shapes=[
            pltpu.VMEM((width // (2 * LANES), 2 * LANES), F32),
            pltpu.VMEM((2, lax.axis_size("y")) + weights[0].shape, BF16),
        ],
        compiler_params=SMALL,
        cost_estimate=pl.CostEstimate(flops=3 * 10**8, bytes_accessed=2 * 10**6, transcendentals=0),
        name="projection",
    )(pages.reshape(-1, WIDE), *weights, norm_gain)
    scaled = scaled.reshape(members * sections, quarter, -1)
    scaled = lax.all_to_all(scaled, ("z", "section"), split_axis=0, concat_axis=0, tiled=True)
    sums = pl.pallas_call(
        term_kernel,
        out_shape=jax.ShapeDtypeStruct((prompt_count, width), BF16),
        scratch_shapes=[pltpu.VMEM((prompt_count, width), F32), pltpu.VMEM((sections, quarter, width), F32)],
        compiler_params=SMALL,
        cost_estimate=pl.CostEstimate(flops=10**8, bytes_accessed=10**6, transcendentals=0),
        name="norm_terms",
    )(scaled.reshape(members, prompt_count, -1), *hidden)
    sums = lax.all_to_all(sums.reshape(sections, quarter, width), "section", split_axis=0, concat_axis=0, tiled=True)
    return (upper_grad.astype(F32) + sums.reshape(prompt_count, width).astype(F32)).astype(BF16)


def swap(piece):
    return lax.ppermute(piece, "core", [(0, 1), (1, 0)])


def turn(piece, axis, k):
    size = lax.axis_size(axis)
    return lax.ppermute(piece, axis, [(i, (i + k) % size) for i in range(size)])


def part_ways(piece, j):
    rows = lax.axis_size("y")
    pairs = [(2 * y + c, (y + (j if c == 0 else rows - j)) % rows * 2 + c) for y in range(rows) for c in range(2)]
    return lax.ppermute(piece, ("y", "core"), pairs)


def hand_over(hidden, k):
    size, here = hidden.shape[0], lax.axis_index("section")
    return turn(lax.dynamic_index_in_dim(hidden, lax.rem(here + k, size), keepdims=False), "section", k)


def collect(pieces, block):
    count = sum(piece.shape[0] for piece in pieces) // block
    return pl.pallas_call(
        collect_kernel,
        out_shape=jax.ShapeDtypeStruct((count, block, WIDE), BF16),
        compiler_params=SMALL,
        cost_estimate=pl.CostEstimate(flops=0, bytes_accessed=10**6, transcendentals=0),
        name="weight_rows",
    )(*pieces)


def body(queries, out_grad, resp_kv, prompt_kv, prompt_hidden, norm_gain, kv_weight, upper_grad, group_list, lengths, owner_map):
    prompt_count, devices = owner_map.shape
    sections = lax.axis_size("section")
    width = prompt_hidden.shape[-1]
    score_grad, own_out, outgoing = attention(
        queries[0], out_grad[0], resp_kv[0], prompt_kv[0], group_list, lengths, owner_map
    )
    hidden = prompt_hidden[0].reshape(sections, prompt_count // sections, width)
    outgoing, weight, hidden = lax.optimization_barrier((outgoing, kv_weight[0], hidden))
    outgoing = outgoing.reshape(devices, -1, WIDE // 2)
    incoming = lax.all_to_all(outgoing, RESP_AXES, split_axis=0, concat_axis=0, tiled=True)
    sibling = swap(weight)
    both, hidden = lax.optimization_barrier((jnp.concatenate([weight, sibling], axis=0), hidden))
    near = [part_ways(both, 1), part_ways(both, 2)]
    layers = [hidden] + [hand_over(hidden, k) for k in range(1, sections)]
    query_out = query_gradient(score_grad, resp_kv[0], prompt_kv[0])
    incoming, both, near, layers, weight, query_out = lax.optimization_barrier(
        (incoming, both, near, layers, weight, query_out)
    )
    pages = pl.pallas_call(
        page_kernel,
        out_shape=jax.ShapeDtypeStruct((lax.axis_size("z"), prompt_count, WIDE), BF16),
        compiler_params=SMALL,
        cost_estimate=pl.CostEstimate(flops=10**8, bytes_accessed=10**6, transcendentals=0),
        name="page_sum",
    )(jnp.repeat(group_list, 2)[None, :], incoming.reshape(-1, WIDE // 2))
    pages = lax.all_to_all(pages, "z", split_axis=0, concat_axis=0, tiled=True)
    near += [part_ways(both, 3), turn(weight, "y", lax.axis_size("y") // 2)]
    near = collect(near, weight.shape[0])
    far = swap(near)
    prompt_out = finish(pages, [weight, sibling, near, far], layers, norm_gain, upper_grad)
    return (query_out[None], own_out[None], prompt_out[None])


def solution(mesh):
    wide = jax.sharding.Mesh(mesh.devices.reshape(8, 8, 2, mesh.shape["section"]), RESP_AXES + ("section",))
    in_specs = (
        P("section", RESP_AXES, None),
        P("section", RESP_AXES, None),
        P("section", RESP_AXES, None),
        P("section", RESP_AXES, None, None),
        P("section", RESP_AXES, None),
        P("section", None),
        P("section", RESP_AXES, None),
        P(RESP_AXES, None),
        P(),
        P(RESP_AXES),
        P(),
    )
    out_specs = (P("section", RESP_AXES, None),) * 3
    return jax.shard_map(body, mesh=wide, in_specs=in_specs, out_specs=out_specs, check_vma=False)
```
